512 devices in a mesh: dp: 64 (over y, z), vocab: 8 (over x, core).
Axes of the slice: x: 4, y: 8, z: 8, core: 2. Of those that a mesh axis runs over, the one named last changes fastest.
Arguments:
- hidden: bfloat16 [16384, 5120], P('dp'), may hold values from -40 to 40
- head_weight: bfloat16 [5120, 6144], P('dp', 'vocab'), may hold values from -1 to 1, as said below
- targets: int32 [16384], P('dp'), may hold values from 0 to 6143
- kept_mask: int32 [16384], P('dp'), may hold values from 0 to 1, as said below
- old_logprob: float32 [16384], P('dp'), as said below
- advantage: float32 [16384], P('dp'), may hold values from -3 to 3
Outputs:
- entropy: float32 [16384], P('dp')
- grad_hidden: float32 [16384, 5120], P('dp', 'vocab')
- grad_head: float32 [5120, 6144], P('dp', 'vocab')
The draws below stay inside these ranges and needn't reach their ends.
Inputs may be any that keep to these rules, and one draw needn't show every extreme that they name: `kept_mask`: among the 256 tokens of one index of dp at most 80 are kept, and one such block keeps exactly 80; every block keeps at least one. Entries of head_weight lie within 6 / sqrt(5120) of zero. `old_logprob`: within 1.5 of -(log(6144) + 0.5).
All inputs are finite; a program needn't handle non-finite values.
Results may differ from the reference program's by a relative error of at most 0.015.
Values may be sent and summed in bfloat16 or wider, within the bound.
No kernel may reach another device: no remote copies, remote signals or barrier semaphores. Data moves between devices by JAX's collectives and lax.ppermute only.
A program may use at most 64 MiB of HBM per device.

```python
import math
import jax
import jax.numpy as jnp
from jax import lax

D = 5120
VOC_DEV = 768
TOK_DEV = 256
KEEP_MOST = 80
TOKENS = 16384
VOCAB = 6144
N_VOCAB = 8


def shared_mask(key):
    key = jax.random.fold_in(key, 101)
    first_key, second_key, third_key = jax.random.split(key, 3)
    blocks = TOKENS // TOK_DEV
    lowest = max(1, TOK_DEV // 10)
    block_ids = jnp.arange(blocks, dtype=jnp.int32)
    rising = lowest + (KEEP_MOST - lowest) * block_ids // max(blocks - 1, 1)
    counts = jnp.clip(rising - jax.random.randint(first_key, (blocks,), 0, 3), 1, KEEP_MOST)
    chosen = jax.random.randint(second_key, (), blocks // 2, blocks)
    counts = jnp.where(block_ids == chosen, KEEP_MOST, counts)
    block_keys = jax.random.split(third_key, blocks)
    orders = jax.vmap(lambda subkey: jax.random.permutation(subkey, TOK_DEV))(block_keys)
    kept_bits = (orders < counts[:, None]).astype(jnp.int32)
    return kept_bits.reshape(TOKENS)


def shared_head(key):
    key = jax.random.fold_in(key, 202)
    values = jnp.clip(jax.random.normal(key, (D, VOCAB), jnp.float32), -6.0, 6.0)
    return values * D ** (-0.5)


def draw_kept_mask(key, part):
    return shared_mask(key)


def draw_head_weight(key, part):
    return shared_head(key).astype(jnp.bfloat16)


def draw_hidden(key, part):
    key = jax.random.fold_in(key, 303)
    keys = jax.random.split(key, 1)
    normal_rows = jnp.clip(jax.random.normal(keys[0], (TOKENS, D), jnp.float32), -6.0, 6.0)
    return jnp.clip(normal_rows, -40.0, 40.0).astype(jnp.bfloat16)


def draw_old_logprob(key, part):
    key = jax.random.fold_in(key, 404)
    centre = -(math.log(VOCAB) + 0.5)
    values = jax.random.uniform(key, (TOKENS,), jnp.float32, centre - 1.5, centre + 1.5)
    return values


def with_ends(values, stream_key, least, top_value):
    shape = values.shape
    place = [jax.random.randint(jax.random.fold_in(stream_key, axis), (), 0, shape[axis]) for axis in range(len(shape))]
    values = values.at[tuple(place)].set(least)
    longest = shape.index(max(shape))
    place[longest] = (place[longest] + 1) % shape[longest]
    return values.at[tuple(place)].set(top_value)


def shard_levels(own_key, dims, pieces, smallest, top_value):
    factor_of, own = 1.0, jax.random.fold_in(own_key, 6)
    for dim, shards_of in pieces:
        heights = jnp.exp(jax.random.uniform(jax.random.fold_in(own, dim), (shards_of,), jnp.float32, smallest / len(pieces), top_value / len(pieces)))
        factor_of = factor_of * jnp.repeat(heights, dims[dim] // shards_of).reshape([-1 if axis == dim else 1 for axis in range(len(dims))])
    return factor_of


def gaussian(rng, shape, spread, most, cuts=(), held_as=jnp.bfloat16):
    gain = shard_levels(rng, shape, cuts, -0.22, 0.18) if cuts else 1.0
    entries = jax.random.normal(rng, shape, jnp.float32) * spread * gain
    return jnp.minimum(jnp.maximum(entries, -most), most).astype(held_as)


def setup_inputs(seed: int = 0) -> dict:
    arg_keys = jax.random.split(jax.random.key(seed), 7)
    hidden = draw_hidden(jax.random.fold_in(arg_keys[6], 71), 0)
    head_weight = draw_head_weight(jax.random.fold_in(arg_keys[6], 71), 0)
    targets = with_ends(jax.random.randint(arg_keys[2], (TOKENS,), 0, VOCAB), jax.random.fold_in(arg_keys[2], 1), 0, VOCAB - 1).astype(jnp.int32)
    kept_mask = draw_kept_mask(jax.random.fold_in(arg_keys[6], 71), 0)
    old_logprob = draw_old_logprob(jax.random.fold_in(arg_keys[6], 71), 0)
    advantage = gaussian(arg_keys[5], (TOKENS,), 1.0, 3.0, ((0, 64),), jnp.float32)
    return dict(hidden=hidden, head_weight=head_weight, targets=targets, kept_mask=kept_mask, old_logprob=old_logprob, advantage=advantage)


clip_eps = 0.2
loss_scale = 8192.0


def surrogate_slope(logprob, old_logprob, advantage, keep_float, kept_total):
    importance = jnp.exp(logprob - old_logprob)
    bent_term = jnp.tanh((importance - 1.0) / clip_eps)
    clipped = 1.0 + clip_eps * bent_term
    choose_grad = jnp.where(importance * advantage <= clipped * advantage, advantage,
                            advantage * (1.0 - bent_term * bent_term))
    return -(loss_scale / kept_total) * keep_float * choose_grad * importance


def reference(hidden, head_weight, targets, kept_mask, old_logprob, advantage):
    logits = jnp.dot(hidden, head_weight, preferred_element_type=jnp.float32)
    row_top = jnp.max(logits, axis=1)
    shifted = logits - row_top[:, None]
    weights = jnp.exp(shifted)
    row_total = jnp.sum(weights, axis=1)
    row_moment = jnp.sum(weights * shifted, axis=1)
    entropy = jnp.log(row_total) - row_moment / row_total
    positions = jnp.arange(VOCAB, dtype=jnp.int32)
    onehot = (positions[None, :] == targets[:, None]).astype(jnp.float32)
    picked = jnp.sum(logits * onehot, axis=1)
    logprob = picked - row_top - jnp.log(row_total)
    keep_float = kept_mask.astype(jnp.float32)
    kept_total = jnp.sum(keep_float)
    logprob_grad = surrogate_slope(logprob, old_logprob, advantage, keep_float, kept_total)
    softmax_rows = jnp.exp(logits - row_top[:, None]) / row_total[:, None]
    logit_grads = (logprob_grad[:, None] * (onehot - softmax_rows)).astype(jnp.bfloat16)
    grad_hidden = jnp.zeros((TOKENS, D), jnp.float32)
    for block in range(N_VOCAB):
        grad_block = logit_grads[:, block * VOC_DEV:(block + 1) * VOC_DEV]
        head_block = head_weight[:, block * VOC_DEV:(block + 1) * VOC_DEV]
        hidden_part = lax.dot_general(grad_block, head_block, (((1,), (1,)), ((), ())),
                                      preferred_element_type=jnp.float32).astype(jnp.bfloat16)
        grad_hidden = grad_hidden + hidden_part.astype(jnp.float32)
    grad_head = jnp.dot(hidden.T, logit_grads, preferred_element_type=jnp.float32)
    return entropy, grad_hidden, grad_head
```

```python
import jax
import jax.numpy as jnp
from jax import lax
from jax.sharding import Mesh, PartitionSpec as P

Y, Z, X, C = 8, 8, 4, 2
V = X * C
SLOTS = 96
CLIP_EPS = 0.2
LOSS_SCALE = 8192.0


def surrogate_slope(logprob, old_logprob, advantage, keep_float):
    importance = jnp.exp(logprob - old_logprob)
    bent_term = jnp.tanh((importance - 1.0) / CLIP_EPS)
    clipped = 1.0 + CLIP_EPS * bent_term
    choose_grad = jnp.where(
        importance * advantage <= clipped * advantage,
        advantage,
        advantage * (1.0 - bent_term * bent_term),
    )
    return keep_float * choose_grad * importance


def to_all(values, axes, n):
    return lax.all_to_all(
        jnp.broadcast_to(values[None], (n,) + values.shape), axes, split_axis=0, concat_axis=0
    )


def per_device(hidden, head_weight, targets, kept_mask, old_logprob, advantage):
    tokens, width = hidden.shape
    rows, cols = head_weight.shape
    offset = (lax.axis_index("x") * C + lax.axis_index("c")) * cols
    assembled = lax.all_gather(head_weight, ("y", "z"), axis=0, tiled=True)

    keep_float = kept_mask.astype(jnp.float32)
    slot_index = jnp.cumsum(kept_mask) - 1
    ids = jnp.arange(SLOTS, dtype=jnp.int32)
    selector = ((slot_index[None, :] == ids[:, None]) & (kept_mask[None, :] == 1)).astype(jnp.bfloat16)
    kept_hidden = jnp.dot(selector, hidden, preferred_element_type=jnp.float32).astype(jnp.bfloat16)
    kept_hidden = kept_hidden.reshape(SLOTS, Y, Z, rows).transpose(2, 0, 1, 3).reshape(Z, SLOTS, Y * rows)
    kept_hidden = lax.all_to_all(kept_hidden, "z", split_axis=0, concat_axis=0)
    kept_hidden = kept_hidden.reshape(Z * SLOTS, Y * rows)
    kept_here = jnp.broadcast_to(jnp.sum(keep_float), (8, 128))
    kept_y = jnp.sum(to_all(kept_here, "y", Y), axis=0)
    kept_total = jnp.sum(to_all(kept_y, "z", Z), axis=0)[0, 0]
    scale = -(LOSS_SCALE / kept_total)

    logits = jnp.dot(hidden, assembled, preferred_element_type=jnp.float32)
    local_target = targets - offset
    positions = jnp.arange(cols, dtype=jnp.int32)
    onehot = (positions[None, :] == local_target[:, None]).astype(jnp.float32)
    local_pick = jnp.sum(logits * onehot, axis=1)
    local_top = jnp.max(logits, axis=1)
    shifted = logits - local_top[:, None]
    weights = jnp.exp(shifted)
    stats = jnp.stack(
        [local_top, jnp.sum(weights, axis=1), jnp.sum(weights * shifted, axis=1), local_pick]
    )
    stats = to_all(stats, ("x", "c"), V)
    tops, totals, moments, picks = (stats[:, i] for i in range(4))
    row_top = jnp.max(tops, axis=0)
    lower = tops - row_top[None]
    factor = jnp.exp(lower)
    row_total = jnp.sum(totals * factor, axis=0)
    row_moment = jnp.sum((moments + lower * totals) * factor, axis=0)
    picked = jnp.sum(picks, axis=0)
    entropy = jnp.log(row_total) - row_moment / row_total
    logprob = picked - row_top - jnp.log(row_total)
    slope = surrogate_slope(logprob, old_logprob, advantage, keep_float)
    softmax_rows = jnp.exp(logits - row_top[:, None]) / row_total[:, None]
    logit_grads = (slope[:, None] * (onehot - softmax_rows)).astype(jnp.bfloat16)
    compact = jnp.dot(selector, logit_grads, preferred_element_type=jnp.float32).astype(jnp.bfloat16)

    all_slots = lax.all_gather(compact, "z", axis=0, tiled=True)
    partial_head = lax.dot_general(
        kept_hidden, all_slots, (((0,), (0,)), ((), ())), preferred_element_type=jnp.float32
    ).astype(jnp.bfloat16)
    parts = lax.all_to_all(partial_head.reshape(Y, rows, cols), "y", split_axis=0, concat_axis=0)
    grad_head = scale * jnp.sum(parts.astype(jnp.float32), axis=0)

    hidden_part = lax.dot_general(
        compact, assembled, (((1,), (1,)), ((), ())), preferred_element_type=jnp.float32
    ).astype(jnp.bfloat16)
    mine = width // V
    hidden_part = hidden_part.reshape(SLOTS, V, mine).transpose(1, 0, 2)
    hidden_part = lax.all_to_all(hidden_part, ("x", "c"), split_axis=0, concat_axis=0)
    spread = jnp.tile(selector, (V, 1))
    grad_hidden = scale * lax.dot_general(
        spread, hidden_part.reshape(V * SLOTS, mine), (((0,), (0,)), ((), ())),
        preferred_element_type=jnp.float32,
    )
    return (entropy, grad_hidden, grad_head)


def solution(mesh):
    grid = Mesh(mesh.devices.reshape(Y, Z, X, C), ("y", "z", "x", "c"))
    dp, vocab = ("y", "z"), ("x", "c")
    placed = (P(dp, None), P(dp, vocab), P(dp), P(dp), P(dp), P(dp))
    return jax.shard_map(
        per_device,
        mesh=grid,
        in_specs=placed,
        out_specs=(P(dp), P(dp, vocab), P(dp, vocab)),
        check_vma=False,
    )
```

```python
import jax
import jax.numpy as jnp
from jax import lax
from jax.sharding import Mesh, PartitionSpec as P

Y, Z, X, C = 8, 8, 4, 2
V = X * C
SLOTS = 96
CLIP_EPS = 0.2
LOSS_SCALE = 8192.0


def surrogate_slope(logprob, old_logprob, advantage, keep_float):
    importance = jnp.exp(logprob - old_logprob)
    bent_term = jnp.tanh((importance - 1.0) / CLIP_EPS)
    clipped = 1.0 + CLIP_EPS * bent_term
    choose_grad = jnp.where(
        importance * advantage <= clipped * advantage,
        advantage,
        advantage * (1.0 - bent_term * bent_term),
    )
    return keep_float * choose_grad * importance


def to_all(values, axes, n):
    return lax.all_to_all(
        jnp.broadcast_to(values[None], (n,) + values.shape), axes, split_axis=0, concat_axis=0
    )


def per_device(hidden, head_weight, targets, kept_mask, old_logprob, advantage):
    tokens, width = hidden.shape
    rows, cols = head_weight.shape
    offset = (lax.axis_index("x") * C + lax.axis_index("c")) * cols
    assembled = lax.all_gather(head_weight, ("y", "z"), axis=0, tiled=True)

    keep_float = kept_mask.astype(jnp.float32)
    slot_index = jnp.cumsum(kept_mask) - 1
    ids = jnp.arange(SLOTS, dtype=jnp.int32)
    selector = ((slot_index[None, :] == ids[:, None]) & (kept_mask[None, :] == 1)).astype(jnp.bfloat16)
    kept_hidden = jnp.dot(selector, hidden, preferred_element_type=jnp.float32).astype(jnp.bfloat16)
    kept_hidden = kept_hidden.reshape(SLOTS, Y, Z, rows).transpose(2, 0, 1, 3).reshape(Z, SLOTS, Y * rows)
    kept_hidden = lax.all_to_all(kept_hidden, "z", split_axis=0, concat_axis=0)
    kept_hidden = kept_hidden.reshape(Z * SLOTS, Y * rows)
    kept_here = jnp.broadcast_to(jnp.sum(keep_float), (8, 128))
    kept_y = jnp.sum(to_all(kept_here, "y", Y), axis=0)
    kept_total = jnp.sum(to_all(kept_y, "z", Z), axis=0)[0, 0]
    scale = -(LOSS_SCALE / kept_total)
    hidden, kept_hidden, scale = lax.optimization_barrier((hidden, kept_hidden, scale))

    logits = jnp.dot(hidden, assembled, preferred_element_type=jnp.float32)
    local_target = targets - offset
    positions = jnp.arange(cols, dtype=jnp.int32)
    onehot = (positions[None, :] == local_target[:, None]).astype(jnp.float32)
    local_pick = jnp.sum(logits * onehot, axis=1)
    local_top = jnp.max(logits, axis=1)
    shifted = logits - local_top[:, None]
    weights = jnp.exp(shifted)
    stats = jnp.stack(
        [local_top, jnp.sum(weights, axis=1), jnp.sum(weights * shifted, axis=1), local_pick]
    )
    stats = to_all(stats, ("x", "c"), V)
    tops, totals, moments, picks = (stats[:, i] for i in range(4))
    row_top = jnp.max(tops, axis=0)
    lower = tops - row_top[None]
    factor = jnp.exp(lower)
    row_total = jnp.sum(totals * factor, axis=0)
    row_moment = jnp.sum((moments + lower * totals) * factor, axis=0)
    picked = jnp.sum(picks, axis=0)
    entropy = jnp.log(row_total) - row_moment / row_total
    logprob = picked - row_top - jnp.log(row_total)
    slope = surrogate_slope(logprob, old_logprob, advantage, keep_float)
    softmax_rows = jnp.exp(logits - row_top[:, None]) / row_total[:, None]
    logit_grads = (slope[:, None] * (onehot - softmax_rows)).astype(jnp.bfloat16)
    compact = jnp.dot(selector, logit_grads, preferred_element_type=jnp.float32).astype(jnp.bfloat16)

    all_slots = lax.all_gather(compact, "z", axis=0, tiled=True)
    partial_head = lax.dot_general(
        kept_hidden, all_slots, (((0,), (0,)), ((), ())), preferred_element_type=jnp.float32
    ).astype(jnp.bfloat16)
    parts = lax.all_to_all(partial_head.reshape(Y, rows, cols), "y", split_axis=0, concat_axis=0)
    grad_head = scale * jnp.sum(parts.astype(jnp.float32), axis=0)

    hidden_part = lax.dot_general(
        compact, assembled, (((1,), (1,)), ((), ())), preferred_element_type=jnp.float32
    ).astype(jnp.bfloat16)
    mine = width // V
    hidden_part = hidden_part.reshape(SLOTS, V, mine).transpose(1, 0, 2)
    hidden_part = lax.all_to_all(hidden_part, ("x", "c"), split_axis=0, concat_axis=0)
    spread = jnp.tile(selector, (V, 1))
    grad_hidden = scale * lax.dot_general(
        spread, hidden_part.reshape(V * SLOTS, mine), (((0,), (0,)), ((), ())),
        preferred_element_type=jnp.float32,
    )
    return (entropy, grad_hidden, grad_head)


def solution(mesh):
    grid = Mesh(mesh.devices.reshape(Y, Z, X, C), ("y", "z", "x", "c"))
    dp, vocab = ("y", "z"), ("x", "c")
    placed = (P(dp, None), P(dp, vocab), P(dp), P(dp), P(dp), P(dp))
    return jax.shard_map(
        per_device,
        mesh=grid,
        in_specs=placed,
        out_specs=(P(dp), P(dp, vocab), P(dp, vocab)),
        check_vma=False,
    )
```

```python
import jax
import jax.numpy as jnp
from jax import lax
from jax.sharding import Mesh, PartitionSpec as P

Y, Z, X, C = 8, 8, 4, 2
V = X * C
KEEP_MOST = 80
SLOTS = 96
CLIP_EPS = 0.2
LOSS_SCALE = 8192.0


def surrogate_slope(logprob, old_logprob, advantage, keep_float):
    importance = jnp.exp(logprob - old_logprob)
    bent_term = jnp.tanh((importance - 1.0) / CLIP_EPS)
    clipped = 1.0 + CLIP_EPS * bent_term
    choose_grad = jnp.where(
        importance * advantage <= clipped * advantage,
        advantage,
        advantage * (1.0 - bent_term * bent_term),
    )
    return keep_float * choose_grad * importance


def exchange(parts, axes):
    return lax.all_to_all(parts, axes, split_axis=0, concat_axis=0)


def to_all(values, axes, n):
    return exchange(jnp.broadcast_to(values[None], (n,) + values.shape), axes)


def shift(block, step):
    return lax.ppermute(block, "z", [(i, (i + step) % Z) for i in range(Z)])


def ring_over_z(own):
    here = lax.axis_index("z")
    whole = jnp.zeros((Y, Z) + own.shape[1:], own.dtype)

    def put(whole, block, away, first=0):
        at = lax.rem(here + away + Z, Z)
        return lax.dynamic_update_slice(whole, block[:, None], (first, at, 0, 0))

    whole = put(whole, own, 0)
    up = down = own
    for hop in range(1, Z // 2):
        up, down = shift(up, 1), shift(down, -1)
        whole = put(put(whole, up, -hop), down, hop)
    half = Y // 2
    up, down = shift(up[:half], 1), shift(down[half:], -1)
    whole = put(whole, up, -(Z // 2))
    return put(whole, down, Z // 2, half)


def per_device(hidden, head_weight, targets, kept_mask, old_logprob, advantage):
    tokens, width = hidden.shape
    rows, cols = head_weight.shape
    half = cols // 2
    offset = (lax.axis_index("x") * C + lax.axis_index("c")) * cols

    head_a = lax.all_gather(head_weight[:, :half], ("y", "z"), axis=0, tiled=True)
    small_b = to_all(head_weight[:, half:], "y", Y)

    keep_float = kept_mask.astype(jnp.float32)
    slot_index = jnp.cumsum(kept_mask) - 1
    ids = jnp.arange(SLOTS, dtype=jnp.int32)
    selector = ((slot_index[None, :] == ids[:, None]) & (kept_mask[None, :] == 1)).astype(jnp.bfloat16)
    hidden_early, small_b = lax.optimization_barrier((hidden, small_b))
    head_b = ring_over_z(small_b).reshape(width, half)
    kept_hidden = jnp.dot(selector, hidden_early, preferred_element_type=jnp.float32)
    kept_hidden = jnp.where(ids[:, None] < KEEP_MOST, kept_hidden, jnp.sum(keep_float)).astype(jnp.bfloat16)
    kept_hidden = exchange(kept_hidden.reshape(SLOTS, Y, Z * rows).transpose(1, 0, 2), "y")
    kept_y = jnp.sum(kept_hidden[:, KEEP_MOST, :128].astype(jnp.float32), axis=0)
    kept_total = jnp.sum(to_all(jnp.broadcast_to(kept_y, (8, 128)), "z", Z), axis=0)[0, 0]
    scale = -(LOSS_SCALE / kept_total)
    hidden, kept_hidden, scale = lax.optimization_barrier((hidden, kept_hidden, scale))

    logits = jnp.concatenate(
        [
            jnp.dot(hidden, head_a, preferred_element_type=jnp.float32),
            jnp.dot(hidden, head_b, preferred_element_type=jnp.float32),
        ],
        axis=1,
    )
    local_target = targets - offset
    positions = jnp.arange(cols, dtype=jnp.int32)
    onehot = (positions[None, :] == local_target[:, None]).astype(jnp.float32)
    local_pick = jnp.sum(logits * onehot, axis=1)
    local_top = jnp.max(logits, axis=1)
    shifted = logits - local_top[:, None]
    weights = jnp.exp(shifted)
    stats = jnp.stack(
        [local_top, jnp.sum(weights, axis=1), jnp.sum(weights * shifted, axis=1), local_pick]
    )
    stats = to_all(stats, ("x", "c"), V)
    tops, totals, moments, picks = (stats[:, i] for i in range(4))
    row_top = jnp.max(tops, axis=0)
    lower = tops - row_top[None]
    factor = jnp.exp(lower)
    row_total = jnp.sum(totals * factor, axis=0)
    row_moment = jnp.sum((moments + lower * totals) * factor, axis=0)
    picked = jnp.sum(picks, axis=0)
    entropy = jnp.log(row_total) - row_moment / row_total
    logprob = picked - row_top - jnp.log(row_total)
    slope = surrogate_slope(logprob, old_logprob, advantage, keep_float)
    softmax_rows = jnp.exp(logits - row_top[:, None]) / row_total[:, None]
    logit_grads = (slope[:, None] * (onehot - softmax_rows)).astype(jnp.bfloat16)
    compact = jnp.dot(selector, logit_grads, preferred_element_type=jnp.float32).astype(jnp.bfloat16)

    all_slots = lax.all_gather(compact, "y", axis=0, tiled=True)
    part_head = lax.dot_general(
        kept_hidden.reshape(Y * SLOTS, Z * rows), all_slots, (((0,), (0,)), ((), ())),
        preferred_element_type=jnp.float32,
    ).astype(jnp.bfloat16)
    sums = exchange(part_head.reshape(Z, rows, cols), "z")
    grad_head = scale * jnp.sum(sums.astype(jnp.float32), axis=0)

    over_cols = (((1,), (1,)), ((), ()))
    hidden_part = (
        lax.dot_general(compact[:, :half], head_a, over_cols, preferred_element_type=jnp.float32)
        + lax.dot_general(compact[:, half:], head_b, over_cols, preferred_element_type=jnp.float32)
    ).astype(jnp.bfloat16)
    mine = width // V
    hidden_part = exchange(hidden_part.reshape(SLOTS, V, mine).transpose(1, 0, 2), ("x", "c"))
    spread = jnp.tile(selector, (V, 1))
    grad_hidden = scale * lax.dot_general(
        spread, hidden_part.reshape(V * SLOTS, mine), (((0,), (0,)), ((), ())),
        preferred_element_type=jnp.float32,
    )
    return (entropy, grad_hidden, grad_head)


def solution(mesh):
    grid = Mesh(mesh.devices.reshape(Y, Z, X, C), ("y", "z", "x", "c"))
    dp, vocab = ("y", "z"), ("x", "c")
    placed = (P(dp, None), P(dp, vocab), P(dp), P(dp), P(dp), P(dp))
    return jax.shard_map(
        per_device,
        mesh=grid,
        in_specs=placed,
        out_specs=(P(dp), P(dp, vocab), P(dp, vocab)),
        check_vma=False,
    )
```

```python
import jax
import jax.numpy as jnp
from jax import lax
from jax.sharding import Mesh, PartitionSpec as P

Y, Z, X, C = 8, 8, 4, 2
V = X * C
KEEP_MOST = 80
SPARE = 8
SLOTS = 96
CLIP_EPS = 0.2
LOSS_SCALE = 8192.0


def surrogate_slope(logprob, old_logprob, advantage, keep_float):
    importance = jnp.exp(logprob - old_logprob)
    bent_term = jnp.tanh((importance - 1.0) / CLIP_EPS)
    clipped = 1.0 + CLIP_EPS * bent_term
    choose_grad = jnp.where(
        importance * advantage <= clipped * advantage,
        advantage,
        advantage * (1.0 - bent_term * bent_term),
    )
    return keep_float * choose_grad * importance


def exchange(parts, axes):
    return lax.all_to_all(parts, axes, split_axis=0, concat_axis=0)


def to_all(values, axes, n):
    return exchange(jnp.broadcast_to(values[None], (n,) + values.shape), axes)


def shift(block, step):
    return lax.ppermute(block, "z", [(i, (i + step) % Z) for i in range(Z)])


def ring_over_z(own):
    here = lax.axis_index("z")
    whole = jnp.zeros((Y, Z) + own.shape[1:], own.dtype)

    def put(whole, block, away, first=0):
        at = lax.rem(here + away + Z, Z)
        return lax.dynamic_update_slice(whole, block[:, None], (first, at, 0, 0))

    whole = put(whole, own, 0)
    up = down = own
    for hop in range(1, Z // 2):
        up, down = shift(up, 1), shift(down, -1)
        whole = put(put(whole, up, -hop), down, hop)
    half = Y // 2
    up, down = shift(up[:half], 1), shift(down[half:], -1)
    whole = put(whole, up, -(Z // 2))
    return put(whole, down, Z // 2, half)


def per_device(hidden, head_weight, targets, kept_mask, old_logprob, advantage):
    tokens, width = hidden.shape
    rows, cols = head_weight.shape
    half = cols // 2
    offset = (lax.axis_index("x") * C + lax.axis_index("c")) * cols

    keep_float = kept_mask.astype(jnp.float32)
    count_rows = jnp.broadcast_to(jnp.sum(keep_float).astype(jnp.bfloat16), (SPARE, cols))
    over_z = lax.all_gather(jnp.concatenate([head_weight, count_rows], axis=0), "z")
    small_b = to_all(head_weight[:, half:], "y", Y)
    head_b = ring_over_z(small_b).reshape(width, half)
    over_z, _ = lax.optimization_barrier((over_z, small_b))
    small_a = over_z[:, :rows, :half].reshape(Z * rows, half)
    head_a = lax.all_gather(small_a, "y", axis=0, tiled=True)
    kept_z = jnp.sum(over_z[:, rows, :128].astype(jnp.float32), axis=0)[0]

    slot_index = jnp.cumsum(kept_mask) - 1
    ids = jnp.arange(SLOTS, dtype=jnp.int32)
    selector = ((slot_index[None, :] == ids[:, None]) & (kept_mask[None, :] == 1)).astype(jnp.bfloat16)
    kept_hidden = jnp.dot(selector, hidden, preferred_element_type=jnp.float32)
    high = jnp.floor(kept_z / 64.0)
    count_pair = jnp.where(ids == KEEP_MOST, high, kept_z - 64.0 * high)
    kept_hidden = jnp.where(ids[:, None] < KEEP_MOST, kept_hidden, count_pair[:, None]).astype(jnp.bfloat16)
    kept_hidden = exchange(kept_hidden.reshape(SLOTS, Y, Z * rows).transpose(1, 0, 2), "y")
    pairs = jnp.sum(kept_hidden[:, KEEP_MOST:KEEP_MOST + 2, 0].astype(jnp.float32), axis=0)
    kept_total = 64.0 * pairs[0] + pairs[1]
    scale = -(LOSS_SCALE / kept_total)
    hidden, kept_hidden, scale = lax.optimization_barrier((hidden, kept_hidden, scale))

    logits = jnp.concatenate(
        [
            jnp.dot(hidden, head_a, preferred_element_type=jnp.float32),
            jnp.dot(hidden, head_b, preferred_element_type=jnp.float32),
        ],
        axis=1,
    )
    local_target = targets - offset
    positions = jnp.arange(cols, dtype=jnp.int32)
    onehot = (positions[None, :] == local_target[:, None]).astype(jnp.float32)
    local_pick = jnp.sum(logits * onehot, axis=1)
    local_top = jnp.max(logits, axis=1)
    shifted = logits - local_top[:, None]
    weights = jnp.exp(shifted)
    stats = jnp.stack(
        [local_top, jnp.sum(weights, axis=1), jnp.sum(weights * shifted, axis=1), local_pick]
    )
    stats = to_all(stats, ("x", "c"), V)
    tops, totals, moments, picks = (stats[:, i] for i in range(4))
    row_top = jnp.max(tops, axis=0)
    lower = tops - row_top[None]
    factor = jnp.exp(lower)
    row_total = jnp.sum(totals * factor, axis=0)
    row_moment = jnp.sum((moments + lower * totals) * factor, axis=0)
    picked = jnp.sum(picks, axis=0)
    entropy = jnp.log(row_total) - row_moment / row_total
    logprob = picked - row_top - jnp.log(row_total)
    slope = surrogate_slope(logprob, old_logprob, advantage, keep_float)
    softmax_rows = jnp.exp(logits - row_top[:, None]) / row_total[:, None]
    logit_grads = (slope[:, None] * (onehot - softmax_rows)).astype(jnp.bfloat16)
    compact = jnp.dot(selector, logit_grads, preferred_element_type=jnp.float32).astype(jnp.bfloat16)

    all_slots = lax.all_gather(compact, "y", axis=0, tiled=True)
    part_head = lax.dot_general(
        kept_hidden.reshape(Y * SLOTS, Z * rows), all_slots, (((0,), (0,)), ((), ())),
        preferred_element_type=jnp.float32,
    ).astype(jnp.bfloat16)
    sums = exchange(part_head.reshape(Z, rows, cols), "z")
    grad_head = scale * jnp.sum(sums.astype(jnp.float32), axis=0)

    over_cols = (((1,), (1,)), ((), ()))
    hidden_part = (
        lax.dot_general(compact[:, :half], head_a, over_cols, preferred_element_type=jnp.float32)
        + lax.dot_general(compact[:, half:], head_b, over_cols, preferred_element_type=jnp.float32)
    ).astype(jnp.bfloat16)
    mine = width // V
    hidden_part = exchange(hidden_part.reshape(SLOTS, V, mine).transpose(1, 0, 2), ("x", "c"))
    spread = jnp.tile(selector, (V, 1))
    grad_hidden = scale * lax.dot_general(
        spread, hidden_part.reshape(V * SLOTS, mine), (((0,), (0,)), ((), ())),
        preferred_element_type=jnp.float32,
    )
    return (entropy, grad_hidden, grad_head)


def solution(mesh):
    grid = Mesh(mesh.devices.reshape(Y, Z, X, C), ("y", "z", "x", "c"))
    dp, vocab = ("y", "z"), ("x", "c")
    placed = (P(dp, None), P(dp, vocab), P(dp), P(dp), P(dp), P(dp))
    return jax.shard_map(
        per_device,
        mesh=grid,
        in_specs=placed,
        out_specs=(P(dp), P(dp, vocab), P(dp, vocab)),
        check_vma=False,
    )
```

```python
import jax
import jax.numpy as jnp
from jax import lax
from jax.sharding import Mesh, PartitionSpec as P

Y, Z, X, C = 8, 8, 4, 2
V = X * C
KEEP_MOST = 80
SLOTS = 96
CLIP_EPS = 0.2
LOSS_SCALE = 8192.0


def surrogate_slope(logprob, old_logprob, advantage, keep_float):
    importance = jnp.exp(logprob - old_logprob)
    bent_term = jnp.tanh((importance - 1.0) / CLIP_EPS)
    clipped = 1.0 + CLIP_EPS * bent_term
    choose_grad = jnp.where(
        importance * advantage <= clipped * advantage,
        advantage,
        advantage * (1.0 - bent_term * bent_term),
    )
    return keep_float * choose_grad * importance


def exchange(parts, axes):
    return lax.all_to_all(parts, axes, split_axis=0, concat_axis=0)


def to_all(values, axes, n):
    return exchange(jnp.broadcast_to(values[None], (n,) + values.shape), axes)


def rows_of(weights, factors):
    positions = lax.broadcasted_iota(jnp.int32, weights.shape, weights.ndim - 1).astype(jnp.float32)
    scale, entry, target = (factors[..., i, :, None] for i in range(3))
    return jnp.where(positions == target, entry, -scale * weights.astype(jnp.float32)).astype(jnp.bfloat16)


def per_device(hidden, head_weight, targets, kept_mask, old_logprob, advantage):
    tokens, width = hidden.shape
    rows, cols = head_weight.shape
    offset = (lax.axis_index("x") * C + lax.axis_index("c")) * cols
    head = lax.all_gather(head_weight, ("y", "z"), axis=0, tiled=True)

    keep_float = kept_mask.astype(jnp.float32)
    slot_index = jnp.cumsum(kept_mask) - 1
    ids = jnp.arange(SLOTS, dtype=jnp.int32)
    chosen = (slot_index[None, :] == ids[:, None]) & (kept_mask[None, :] == 1)
    selector = chosen.astype(jnp.bfloat16)
    kept_hidden = jnp.dot(selector, hidden, preferred_element_type=jnp.float32)
    kept_hidden = jnp.where(ids[:, None] < KEEP_MOST, kept_hidden, jnp.sum(keep_float)).astype(jnp.bfloat16)
    kept_hidden = exchange(kept_hidden.reshape(SLOTS, Y, Z * rows).transpose(1, 0, 2), "y")
    kept_y = jnp.sum(kept_hidden[:, KEEP_MOST, :128].astype(jnp.float32), axis=0)
    kept_total = jnp.sum(to_all(jnp.broadcast_to(kept_y, (8, 128)), "z", Z), axis=0)[0, 0]
    scale = -(LOSS_SCALE / kept_total)
    hidden, kept_hidden, scale = lax.optimization_barrier((hidden, kept_hidden, scale))

    logits = jnp.dot(hidden, head, preferred_element_type=jnp.float32)
    local_target = targets - offset
    positions = jnp.arange(cols, dtype=jnp.int32)
    hit = positions[None, :] == local_target[:, None]
    local_top = jnp.max(logits, axis=1)
    shifted = logits - local_top[:, None]
    weights = jnp.exp(shifted)

    compact = jnp.dot(
        selector, jnp.where(hit, 0.0, weights).astype(jnp.bfloat16), preferred_element_type=jnp.float32
    ).astype(jnp.bfloat16)
    all_slots = lax.all_gather(compact, "y")

    stats = jnp.stack(
        [
            local_top,
            jnp.sum(weights, axis=1),
            jnp.sum(weights * shifted, axis=1),
            jnp.sum(jnp.where(hit, logits, 0.0), axis=1),
        ]
    )
    stats = to_all(stats, ("x", "c"), V)
    tops, totals, moments, picks = (stats[:, i] for i in range(4))
    row_top = jnp.max(tops, axis=0)
    lower = tops - row_top[None]
    factor = jnp.exp(lower)
    row_total = jnp.sum(totals * factor, axis=0)
    row_moment = jnp.sum((moments + lower * totals) * factor, axis=0)
    picked = jnp.sum(picks, axis=0)
    entropy = jnp.log(row_total) - row_moment / row_total
    logprob = picked - row_top - jnp.log(row_total)
    slope = surrogate_slope(logprob, old_logprob, advantage, keep_float)
    row_scale = slope * (jnp.exp(local_top - row_top) / row_total)
    row_entry = slope * (1.0 - jnp.exp(picked - row_top) / row_total)
    of_slots = jnp.stack([row_scale, row_entry, local_target.astype(jnp.float32)])
    of_slots = jnp.sum(jnp.where(chosen[None], of_slots[:, None, :], 0.0), axis=2)

    own_rows = rows_of(compact, of_slots)
    hidden_part = lax.dot_general(
        own_rows, head, (((1,), (1,)), ((), ())), preferred_element_type=jnp.float32
    ).astype(jnp.bfloat16)
    mine = width // V
    hidden_part = hidden_part.reshape(SLOTS, V, mine).transpose(1, 0, 2)
    hidden_part, of_slots = lax.optimization_barrier((hidden_part, of_slots))
    hidden_part = exchange(hidden_part, ("x", "c"))

    all_factors = lax.all_gather(jnp.pad(of_slots, ((0, 5), (0, 128 - SLOTS))), "y")
    all_rows = rows_of(all_slots, all_factors[:, :3, :SLOTS])
    part_head = lax.dot_general(
        kept_hidden.reshape(Y * SLOTS, Z * rows), all_rows.reshape(Y * SLOTS, cols), (((0,), (0,)), ((), ())),
        preferred_element_type=jnp.float32,
    ).astype(jnp.bfloat16)
    sums = exchange(part_head.reshape(Z, rows, cols), "z")
    grad_head = scale * jnp.sum(sums.astype(jnp.float32), axis=0)

    spread = jnp.tile(selector, (V, 1))
    grad_hidden = scale * lax.dot_general(
        spread, hidden_part.reshape(V * SLOTS, mine), (((0,), (0,)), ((), ())),
        preferred_element_type=jnp.float32,
    )
    return (entropy, grad_hidden, grad_head)


def solution(mesh):
    grid = Mesh(mesh.devices.reshape(Y, Z, X, C), ("y", "z", "x", "c"))
    dp, vocab = ("y", "z"), ("x", "c")
    placed = (P(dp, None), P(dp, vocab), P(dp), P(dp), P(dp), P(dp))
    return jax.shard_map(
        per_device,
        mesh=grid,
        in_specs=placed,
        out_specs=(P(dp), P(dp, vocab), P(dp, vocab)),
        check_vma=False,
    )
```

```python
import jax
import jax.numpy as jnp
from jax import lax
from jax.sharding import Mesh, PartitionSpec as P

Y, Z, X, C = 8, 8, 4, 2
V = X * C
KEEP_MOST = 80
SPARE = 16
CLIP_EPS = 0.2
LOSS_SCALE = 8192.0


def surrogate_slope(logprob, old_logprob, advantage, keep_float):
    importance = jnp.exp(logprob - old_logprob)
    bent_term = jnp.tanh((importance - 1.0) / CLIP_EPS)
    clipped = 1.0 + CLIP_EPS * bent_term
    choose_grad = jnp.where(
        importance * advantage <= clipped * advantage,
        advantage,
        advantage * (1.0 - bent_term * bent_term),
    )
    return keep_float * choose_grad * importance


def exchange(parts, axes):
    return lax.all_to_all(parts, axes, split_axis=0, concat_axis=0)


def to_all(values, axes, n):
    return exchange(jnp.broadcast_to(values[None], (n,) + values.shape), axes)


def shift(block, step):
    return lax.ppermute(block, "z", [(i, (i + step) % Z) for i in range(Z)])


def ring_over_z(own):
    here = lax.axis_index("z")
    whole = jnp.zeros((Y, Z) + own.shape[1:], own.dtype)

    def put(whole, block, away):
        at = lax.rem(here + (away + Z), Z)
        return lax.dynamic_update_slice(whole, block[:, None], (0, at, 0, 0))

    whole = put(whole, own, 0)
    up = down = own
    for hop in range(1, Z // 2 + 1):
        down = shift(down, -1)
        whole = put(whole, down, hop)
        if hop < Z // 2:
            up = shift(up, 1)
            whole = put(whole, up, -hop)
    return whole


def per_device(hidden, head_weight, targets, kept_mask, old_logprob, advantage):
    tokens, width = hidden.shape
    rows, cols = head_weight.shape
    half = cols // 2
    offset = (lax.axis_index("x") * C + lax.axis_index("c")) * cols

    keep_float = kept_mask.astype(jnp.float32)
    count_rows = jnp.broadcast_to(jnp.sum(keep_float).astype(jnp.bfloat16), (SPARE, half))
    over_z = to_all(jnp.concatenate([head_weight[:, :half], count_rows], axis=0), "z", Z)
    head_a = lax.all_gather(over_z[:, :rows].reshape(Z * rows, half), "y", axis=0, tiled=True)
    kept_z = jnp.sum(over_z[:, rows, :128].astype(jnp.float32), axis=0)[0]
    head_of_b, _ = lax.optimization_barrier((head_weight[:, half:], over_z))
    small_b = to_all(head_of_b, "y", Y)
    head_b = ring_over_z(small_b).reshape(width, half)

    slot_index = jnp.cumsum(kept_mask) - 1
    ids = jnp.arange(KEEP_MOST, dtype=jnp.int32)
    selector = ((slot_index[None, :] == ids[:, None]) & (kept_mask[None, :] == 1)).astype(jnp.bfloat16)
    kept_hidden = jnp.dot(selector, hidden, preferred_element_type=jnp.float32).astype(jnp.bfloat16)
    kept_hidden = kept_hidden.reshape(KEEP_MOST, Y, Z * rows).transpose(1, 0, 2)
    high = jnp.floor(kept_z / 64.0)
    count_pair = jnp.where(jnp.arange(SPARE) == 0, high, kept_z - 64.0 * high).astype(jnp.bfloat16)
    count_pair = jnp.broadcast_to(count_pair[None, :, None], (Y, SPARE, Z * rows))
    kept_hidden, _ = lax.optimization_barrier((kept_hidden, small_b))
    kept_hidden = exchange(jnp.concatenate([kept_hidden, count_pair], axis=1), "y")
    pairs = jnp.sum(kept_hidden[:, KEEP_MOST:, 0].astype(jnp.float32), axis=0)
    kept_total = 64.0 * pairs[0] + pairs[1]
    kept_hidden = kept_hidden[:, :KEEP_MOST]
    scale = -(LOSS_SCALE / kept_total)
    hidden, kept_hidden, scale = lax.optimization_barrier((hidden, kept_hidden, scale))

    logits = jnp.concatenate(
        [
            jnp.dot(hidden, head_a, preferred_element_type=jnp.float32),
            jnp.dot(hidden, head_b, preferred_element_type=jnp.float32),
        ],
        axis=1,
    )
    local_target = targets - offset
    positions = jnp.arange(cols, dtype=jnp.int32)
    onehot = (positions[None, :] == local_target[:, None]).astype(jnp.float32)
    local_pick = jnp.sum(logits * onehot, axis=1)
    local_top = jnp.max(logits, axis=1)
    shifted = logits - local_top[:, None]
    weights = jnp.exp(shifted)
    stats = jnp.stack(
        [local_top, jnp.sum(weights, axis=1), jnp.sum(weights * shifted, axis=1), local_pick]
    )
    stats = to_all(stats, ("x", "c"), V)
    tops, totals, moments, picks = (stats[:, i] for i in range(4))
    row_top = jnp.max(tops, axis=0)
    lower = tops - row_top[None]
    factor = jnp.exp(lower)
    row_total = jnp.sum(totals * factor, axis=0)
    row_moment = jnp.sum((moments + lower * totals) * factor, axis=0)
    picked = jnp.sum(picks, axis=0)
    entropy = jnp.log(row_total) - row_moment / row_total
    logprob = picked - row_top - jnp.log(row_total)
    slope = surrogate_slope(logprob, old_logprob, advantage, keep_float)
    softmax_rows = jnp.exp(logits - row_top[:, None]) / row_total[:, None]
    logit_grads = (slope[:, None] * (onehot - softmax_rows)).astype(jnp.bfloat16)
    compact = jnp.dot(selector, logit_grads, preferred_element_type=jnp.float32).astype(jnp.bfloat16)

    all_slots = to_all(compact, "y", Y)
    part_head = lax.dot_general(
        kept_hidden.reshape(Y * KEEP_MOST, Z * rows), all_slots.reshape(Y * KEEP_MOST, cols),
        (((0,), (0,)), ((), ())), preferred_element_type=jnp.float32,
    ).astype(jnp.bfloat16)
    sums = exchange(part_head.reshape(Z, rows, cols), "z")
    grad_head = scale * jnp.sum(sums.astype(jnp.float32), axis=0)

    over_cols = (((1,), (1,)), ((), ()))
    hidden_part = (
        lax.dot_general(compact[:, :half], head_a, over_cols, preferred_element_type=jnp.float32)
        + lax.dot_general(compact[:, half:], head_b, over_cols, preferred_element_type=jnp.float32)
    ).astype(jnp.bfloat16)
    mine = width // V
    hidden_part = hidden_part.reshape(KEEP_MOST, V, mine).transpose(1, 0, 2)
    hidden_part = lax.psum_scatter(hidden_part, ("x", "c"), scatter_dimension=0)
    grad_hidden = scale * lax.dot_general(
        selector, hidden_part, (((0,), (0,)), ((), ())), preferred_element_type=jnp.float32
    )
    return (entropy, grad_hidden, grad_head)


def solution(mesh):
    grid = Mesh(mesh.devices.reshape(Y, Z, X, C), ("y", "z", "x", "c"))
    dp, vocab = ("y", "z"), ("x", "c")
    placed = (P(dp, None), P(dp, vocab), P(dp), P(dp), P(dp), P(dp))
    return jax.shard_map(
        per_device,
        mesh=grid,
        in_specs=placed,
        out_specs=(P(dp), P(dp, vocab), P(dp, vocab)),
        check_vma=False,
    )
```

```python
import jax
import jax.numpy as jnp
from jax import lax
from jax.sharding import Mesh, PartitionSpec as P

Y, Z, X, C = 8, 8, 4, 2
V = X * C
KEEP_MOST = 80
SPARE = 16
SLOTS = KEEP_MOST + SPARE
SENT = 512
CLIP_EPS = 0.2
LOSS_SCALE = 8192.0


def surrogate_slope(logprob, old_logprob, advantage, keep_float):
    importance = jnp.exp(logprob - old_logprob)
    bent_term = jnp.tanh((importance - 1.0) / CLIP_EPS)
    clipped = 1.0 + CLIP_EPS * bent_term
    choose_grad = jnp.where(
        importance * advantage <= clipped * advantage,
        advantage,
        advantage * (1.0 - bent_term * bent_term),
    )
    return keep_float * choose_grad * importance


def exchange(parts, axes):
    return lax.all_to_all(parts, axes, split_axis=0, concat_axis=0)


def to_all(values, axes, n):
    return exchange(jnp.broadcast_to(values[None], (n,) + values.shape), axes)


def shift(block, step):
    return lax.ppermute(block, "y", [(i, (i + step) % Y) for i in range(Y)])


def ring_over_y(own):
    here = lax.axis_index("y")
    whole = jnp.zeros((Y,) + own.shape, own.dtype)

    def put(whole, block, away):
        return lax.dynamic_update_slice(whole, block[None], (lax.rem(here + (away + Y), Y), 0, 0))

    whole = put(whole, own, 0)
    up = down = own
    for hop in range(1, Y // 2 + 1):
        down = shift(down, -1)
        whole = put(whole, down, hop)
        if hop < Y // 2:
            up = shift(up, 1)
            whole = put(whole, up, -hop)
    return whole


def rows_of(weights, factors):
    positions = lax.broadcasted_iota(jnp.int32, weights.shape, weights.ndim - 1).astype(jnp.float32)
    scale, entry, target = (factors[..., i, :, None] for i in range(3))
    return jnp.where(positions == target, entry, -scale * weights.astype(jnp.float32)).astype(jnp.bfloat16)


def per_device(hidden, head_weight, targets, kept_mask, old_logprob, advantage):
    tokens, width = hidden.shape
    rows, cols = head_weight.shape
    offset = (lax.axis_index("x") * C + lax.axis_index("c")) * cols

    head_a = lax.all_gather(head_weight[:, :SENT], ("y", "z"), axis=0, tiled=True)
    keep_float = kept_mask.astype(jnp.float32)
    count_rows = jnp.broadcast_to(jnp.sum(keep_float).astype(jnp.bfloat16), (SPARE, cols - SENT))
    over_z = to_all(jnp.concatenate([head_weight[:, SENT:], count_rows], axis=0), "z", Z)
    kept_z = jnp.sum(over_z[:, rows, :128].astype(jnp.float32), axis=0)[0]
    small_b = over_z[:, :rows].reshape(Z * rows, cols - SENT)
    head_b = ring_over_y(small_b).reshape(width, cols - SENT)

    slot_index = jnp.cumsum(kept_mask) - 1
    ids = jnp.arange(SLOTS, dtype=jnp.int32)
    chosen = (slot_index[None, :] == ids[:, None]) & (kept_mask[None, :] == 1)
    selector = chosen.astype(jnp.bfloat16)
    kept_hidden = jnp.dot(selector, hidden, preferred_element_type=jnp.float32)
    high = jnp.floor(kept_z / 64.0)
    count_pair = jnp.where(ids == KEEP_MOST, high, kept_z - 64.0 * high)
    kept_hidden = jnp.where(ids[:, None] < KEEP_MOST, kept_hidden, count_pair[:, None]).astype(jnp.bfloat16)
    kept_hidden = exchange(kept_hidden.reshape(SLOTS, Y, Z * rows).transpose(1, 0, 2), "y")
    pairs = jnp.sum(kept_hidden[:, KEEP_MOST:KEEP_MOST + 2, 0].astype(jnp.float32), axis=0)
    kept_total = 64.0 * pairs[0] + pairs[1]
    scale = -(LOSS_SCALE / kept_total)
    hidden, kept_hidden, scale = lax.optimization_barrier((hidden, kept_hidden, scale))

    logits = jnp.concatenate(
        [
            jnp.dot(hidden, head_a, preferred_element_type=jnp.float32),
            jnp.dot(hidden, head_b, preferred_element_type=jnp.float32),
        ],
        axis=1,
    )
    local_target = targets - offset
    positions = jnp.arange(cols, dtype=jnp.int32)
    hit = positions[None, :] == local_target[:, None]
    local_top = jnp.max(logits, axis=1)
    shifted = logits - local_top[:, None]
    weights = jnp.exp(shifted)

    compact = jnp.dot(
        selector, jnp.where(hit, 0.0, weights).astype(jnp.bfloat16), preferred_element_type=jnp.float32
    ).astype(jnp.bfloat16)
    all_slots = lax.all_gather(compact, "y")

    stats = jnp.stack(
        [
            local_top,
            jnp.sum(weights, axis=1),
            jnp.sum(weights * shifted, axis=1),
            jnp.sum(jnp.where(hit, logits, 0.0), axis=1),
        ]
    )
    stats, compact = lax.optimization_barrier((stats, compact))
    stats = to_all(stats, ("x", "c"), V)
    tops, totals, moments, picks = (stats[:, i] for i in range(4))
    row_top = jnp.max(tops, axis=0)
    lower = tops - row_top[None]
    factor = jnp.exp(lower)
    row_total = jnp.sum(totals * factor, axis=0)
    row_moment = jnp.sum((moments + lower * totals) * factor, axis=0)
    picked = jnp.sum(picks, axis=0)
    entropy = jnp.log(row_total) - row_moment / row_total
    logprob = picked - row_top - jnp.log(row_total)
    slope = surrogate_slope(logprob, old_logprob, advantage, keep_float)
    row_scale = slope * (jnp.exp(local_top - row_top) / row_total)
    row_entry = slope * (1.0 - jnp.exp(picked - row_top) / row_total)
    of_slots = jnp.stack([row_scale, row_entry, local_target.astype(jnp.float32)])
    of_slots = jnp.sum(jnp.where(chosen[None], of_slots[:, None, :], 0.0), axis=2)

    all_factors = to_all(jnp.pad(of_slots, ((0, 5), (0, 128 - SLOTS))), "y", Y)

    own_rows = rows_of(compact, of_slots)
    over_cols = (((1,), (1,)), ((), ()))
    hidden_part = (
        lax.dot_general(own_rows[:, :SENT], head_a, over_cols, preferred_element_type=jnp.float32)
        + lax.dot_general(own_rows[:, SENT:], head_b, over_cols, preferred_element_type=jnp.float32)
    ).astype(jnp.bfloat16)
    mine = width // V
    hidden_part = hidden_part.reshape(SLOTS, V, mine).transpose(1, 0, 2)
    hidden_part, all_factors = lax.optimization_barrier((hidden_part, all_factors))
    hidden_part = exchange(hidden_part, ("x", "c"))

    all_rows = rows_of(all_slots, all_factors[:, :3, :SLOTS])
    part_head = lax.dot_general(
        kept_hidden.reshape(Y * SLOTS, Z * rows), all_rows.reshape(Y * SLOTS, cols), (((0,), (0,)), ((), ())),
        preferred_element_type=jnp.float32,
    ).astype(jnp.bfloat16)
    sums = exchange(part_head.reshape(Z, rows, cols), "z")
    grad_head = scale * jnp.sum(sums.astype(jnp.float32), axis=0)

    spread = jnp.tile(selector, (V, 1))
    grad_hidden = scale * lax.dot_general(
        spread, hidden_part.reshape(V * SLOTS, mine), (((0,), (0,)), ((), ())),
        preferred_element_type=jnp.float32,
    )
    return (entropy, grad_hidden, grad_head)


def solution(mesh):
    grid = Mesh(mesh.devices.reshape(Y, Z, X, C), ("y", "z", "x", "c"))
    dp, vocab = ("y", "z"), ("x", "c")
    placed = (P(dp, None), P(dp, vocab), P(dp), P(dp), P(dp), P(dp))
    return jax.shard_map(
        per_device,
        mesh=grid,
        in_specs=placed,
        out_specs=(P(dp), P(dp, vocab), P(dp, vocab)),
        check_vma=False,
    )
```

```python
import jax
import jax.numpy as jnp
from jax import lax
from jax.sharding import Mesh, PartitionSpec as P

Y, Z, X, C = 8, 8, 4, 2
V = X * C
KEEP_MOST = 80
SPARE = 16
SLOTS = KEEP_MOST + SPARE
SHARE = KEEP_MOST // V
SENT = 512
CLIP_EPS = 0.2
LOSS_SCALE = 8192.0


def surrogate_slope(logprob, old_logprob, advantage, keep_float):
    importance = jnp.exp(logprob - old_logprob)
    bent_term = jnp.tanh((importance - 1.0) / CLIP_EPS)
    clipped = 1.0 + CLIP_EPS * bent_term
    choose_grad = jnp.where(
        importance * advantage <= clipped * advantage,
        advantage,
        advantage * (1.0 - bent_term * bent_term),
    )
    return keep_float * choose_grad * importance


def exchange(parts, axes):
    return lax.all_to_all(parts, axes, split_axis=0, concat_axis=0)


def to_all(values, axes, n):
    return exchange(jnp.broadcast_to(values[None], (n,) + values.shape), axes)


def shift(block, step):
    return lax.ppermute(block, "y", [(i, (i + step) % Y) for i in range(Y)])


def ring_over_y(own):
    here = lax.axis_index("y")
    whole = jnp.zeros((Y,) + own.shape, own.dtype)

    def put(whole, block, away):
        return lax.dynamic_update_slice(whole, block[None], (lax.rem(here + (away + Y), Y), 0, 0))

    whole = put(whole, own, 0)
    up = down = own
    for hop in range(1, Y // 2 + 1):
        down = shift(down, -1)
        whole = put(whole, down, hop)
        if hop < Y // 2:
            up = shift(up, 1)
            whole = put(whole, up, -hop)
    return whole


def rows_of(weights, factors):
    positions = lax.broadcasted_iota(jnp.int32, weights.shape, weights.ndim - 1).astype(jnp.float32)
    scale, entry, target = (factors[..., i, :, None] for i in range(3))
    return jnp.where(positions == target, entry, -scale * weights.astype(jnp.float32)).astype(jnp.bfloat16)


def per_device(hidden, head_weight, targets, kept_mask, old_logprob, advantage):
    tokens, width = hidden.shape
    rows, cols = head_weight.shape
    offset = (lax.axis_index("x") * C + lax.axis_index("c")) * cols

    head_a = lax.all_gather(head_weight[:, :SENT], ("y", "z"), axis=0, tiled=True)
    keep_float = kept_mask.astype(jnp.float32)
    count_rows = jnp.broadcast_to(jnp.sum(keep_float).astype(jnp.bfloat16), (SPARE, cols - SENT))
    over_z = to_all(jnp.concatenate([head_weight[:, SENT:], count_rows], axis=0), "z", Z)
    kept_z = jnp.sum(over_z[:, rows, :128].astype(jnp.float32), axis=0)[0]
    small_b = over_z[:, :rows].reshape(Z * rows, cols - SENT)
    head_b = ring_over_y(small_b).reshape(width, cols - SENT)

    slot_index = jnp.cumsum(kept_mask) - 1
    ids = jnp.arange(SLOTS, dtype=jnp.int32)
    chosen = (slot_index[None, :] == ids[:, None]) & (kept_mask[None, :] == 1)
    selector = chosen.astype(jnp.bfloat16)
    share_ids = jnp.arange(SPARE, dtype=jnp.int32)
    first = (lax.axis_index("x") * C + lax.axis_index("c")) * SHARE
    own = (slot_index[None, :] == (first + share_ids)[:, None]) & (kept_mask[None, :] == 1) & (share_ids < SHARE)[:, None]
    kept_hidden = jnp.dot(own.astype(jnp.bfloat16), hidden, preferred_element_type=jnp.float32)
    high = jnp.floor(kept_z / 64.0)
    count_pair = jnp.where(share_ids == SHARE, high, kept_z - 64.0 * high)
    kept_hidden = jnp.where(share_ids[:, None] < SHARE, kept_hidden, count_pair[:, None]).astype(jnp.bfloat16)
    kept_hidden = exchange(kept_hidden.reshape(SPARE, Y, Z * rows).transpose(1, 0, 2), "y")
    pairs = jnp.sum(kept_hidden[:, SHARE:SHARE + 2, 0].astype(jnp.float32), axis=0)
    kept_total = 64.0 * pairs[0] + pairs[1]
    kept_hidden = to_all(kept_hidden, ("x", "c"), V)[:, :, :SHARE]
    kept_hidden = kept_hidden.transpose(1, 0, 2, 3).reshape(Y, KEEP_MOST, Z * rows)
    kept_hidden = jnp.pad(kept_hidden, ((0, 0), (0, SPARE), (0, 0)))
    scale = -(LOSS_SCALE / kept_total)
    hidden, kept_hidden, scale = lax.optimization_barrier((hidden, kept_hidden, scale))

    logits = jnp.concatenate(
        [
            jnp.dot(hidden, head_a, preferred_element_type=jnp.float32),
            jnp.dot(hidden, head_b, preferred_element_type=jnp.float32),
        ],
        axis=1,
    )
    local_target = targets - offset
    positions = jnp.arange(cols, dtype=jnp.int32)
    hit = positions[None, :] == local_target[:, None]
    local_top = jnp.max(logits, axis=1)
    shifted = logits - local_top[:, None]
    weights = jnp.exp(shifted)

    compact = jnp.dot(
        selector, jnp.where(hit, 0.0, weights).astype(jnp.bfloat16), preferred_element_type=jnp.float32
    ).astype(jnp.bfloat16)
    all_slots = lax.all_gather(compact, "y")

    stats = jnp.stack(
        [
            local_top,
            jnp.sum(weights, axis=1),
            jnp.sum(weights * shifted, axis=1),
            jnp.sum(jnp.where(hit, logits, 0.0), axis=1),
        ]
    )
    stats, compact = lax.optimization_barrier((stats, compact))
    stats = to_all(stats, ("x", "c"), V)
    tops, totals, moments, picks = (stats[:, i] for i in range(4))
    row_top = jnp.max(tops, axis=0)
    lower = tops - row_top[None]
    factor = jnp.exp(lower)
    row_total = jnp.sum(totals * factor, axis=0)
    row_moment = jnp.sum((moments + lower * totals) * factor, axis=0)
    picked = jnp.sum(picks, axis=0)
    entropy = jnp.log(row_total) - row_moment / row_total
    logprob = picked - row_top - jnp.log(row_total)
    slope = surrogate_slope(logprob, old_logprob, advantage, keep_float)
    row_scale = slope * (jnp.exp(local_top - row_top) / row_total)
    row_entry = slope * (1.0 - jnp.exp(picked - row_top) / row_total)
    of_slots = jnp.stack([row_scale, row_entry, local_target.astype(jnp.float32)])
    of_slots = jnp.sum(jnp.where(chosen[None], of_slots[:, None, :], 0.0), axis=2)

    all_factors = to_all(jnp.pad(of_slots, ((0, 5), (0, 128 - SLOTS))), "y", Y)

    own_rows = rows_of(compact, of_slots)
    over_cols = (((1,), (1,)), ((), ()))
    hidden_part = (
        lax.dot_general(own_rows[:, :SENT], head_a, over_cols, preferred_element_type=jnp.float32)
        + lax.dot_general(own_rows[:, SENT:], head_b, over_cols, preferred_element_type=jnp.float32)
    ).astype(jnp.bfloat16)
    mine = width // V
    hidden_part = hidden_part.reshape(SLOTS, V, mine).transpose(1, 0, 2)
    hidden_part, all_factors = lax.optimization_barrier((hidden_part, all_factors))
    hidden_part = exchange(hidden_part, ("x", "c"))

    all_rows = rows_of(all_slots, all_factors[:, :3, :SLOTS])
    part_head = lax.dot_general(
        kept_hidden.reshape(Y * SLOTS, Z * rows), all_rows.reshape(Y * SLOTS, cols), (((0,), (0,)), ((), ())),
        preferred_element_type=jnp.float32,
    ).astype(jnp.bfloat16)
    sums = exchange(part_head.reshape(Z, rows, cols), "z")
    grad_head = jnp.sum(scale * sums.astype(jnp.float32), axis=0)

    spread = jnp.tile(selector, (V, 1))
    grad_hidden = scale * lax.dot_general(
        spread, hidden_part.reshape(V * SLOTS, mine), (((0,), (0,)), ((), ())),
        preferred_element_type=jnp.float32,
    )
    return (entropy, grad_hidden, grad_head)


def solution(mesh):
    grid = Mesh(mesh.devices.reshape(Y, Z, X, C), ("y", "z", "x", "c"))
    dp, vocab = ("y", "z"), ("x", "c")
    placed = (P(dp, None), P(dp, vocab), P(dp), P(dp), P(dp), P(dp))
    return jax.shard_map(
        per_device,
        mesh=grid,
        in_specs=placed,
        out_specs=(P(dp), P(dp, vocab), P(dp, vocab)),
        check_vma=False,
    )
```

```python
import jax
import jax.numpy as jnp
from jax import lax
from jax.sharding import Mesh, PartitionSpec as P

Y, Z, X, C = 8, 8, 4, 2
V = X * C
KEEP_MOST = 80
SPARE = 16
SHARE = KEEP_MOST // V
CLIP_EPS = 0.2
LOSS_SCALE = 8192.0


def surrogate_slope(logprob, old_logprob, advantage, keep_float):
    importance = jnp.exp(logprob - old_logprob)
    bent_term = jnp.tanh((importance - 1.0) / CLIP_EPS)
    clipped = 1.0 + CLIP_EPS * bent_term
    choose_grad = jnp.where(
        importance * advantage <= clipped * advantage,
        advantage,
        advantage * (1.0 - bent_term * bent_term),
    )
    return keep_float * choose_grad * importance


def exchange(parts, axes):
    return lax.all_to_all(parts, axes, split_axis=0, concat_axis=0)


def to_all(values, axes, n):
    return exchange(jnp.broadcast_to(values[None], (n,) + values.shape), axes)


def ring(own, axis, n):
    blocks = [(0, own)]
    up = down = own
    for hop in range(1, n // 2 + 1):
        down = lax.ppermute(down, axis, [(i, (i - 1) % n) for i in range(n)])
        blocks.append((hop, down))
        if hop < n // 2:
            up = lax.ppermute(up, axis, [(i, (i + 1) % n) for i in range(n)])
            blocks.append((-hop, up))
    return blocks


def per_device(hidden, head_weight, targets, kept_mask, old_logprob, advantage):
    tokens, width = hidden.shape
    rows, cols = head_weight.shape
    half = cols // 2
    at_y, at_z, at_x, at_c = (lax.axis_index(name) for name in ("y", "z", "x", "c"))
    at_v = at_x * C + at_c
    offset = at_v * cols
    across_rows = (((1,), (0,)), ((), ()))

    keep_float = kept_mask.astype(jnp.float32)
    count_rows = jnp.broadcast_to(jnp.sum(keep_float).astype(jnp.bfloat16), (SPARE, half))
    over_z = to_all(jnp.concatenate([head_weight[:, :half], count_rows], axis=0), "z", Z)
    kept_z = jnp.sum(over_z[:, rows, :128].astype(jnp.float32), axis=0)[0]
    head_of_b, _ = lax.optimization_barrier((head_weight[:, half:], over_z))
    over_y = to_all(head_of_b, "y", Y)
    blocks_a = ring(over_z[:, :rows].reshape(Z * rows, half), "y", Y)
    blocks_b = ring(over_y.reshape(Y * rows, half), "z", Z)

    hidden_a = hidden.reshape(tokens, Y, Z * rows).transpose(1, 0, 2)
    hidden_b = hidden.reshape(tokens, Y, Z, rows).transpose(2, 0, 1, 3).reshape(Z, tokens, Y * rows)

    slot_index = jnp.cumsum(kept_mask) - 1
    ids = jnp.arange(KEEP_MOST, dtype=jnp.int32)
    kept = kept_mask[None, :] == 1
    selector = ((slot_index[None, :] == ids[:, None]) & kept).astype(jnp.bfloat16)
    share_ids = jnp.arange(SPARE, dtype=jnp.int32)
    own = (slot_index[None, :] == (at_v * SHARE + share_ids)[:, None]) & kept & (share_ids < SHARE)[:, None]
    kept_share = jnp.dot(own.astype(jnp.bfloat16), hidden, preferred_element_type=jnp.float32)
    high = jnp.floor(kept_z / 64.0)
    count_pair = jnp.where(share_ids == SHARE, high, kept_z - 64.0 * high)
    kept_share = jnp.where(share_ids[:, None] < SHARE, kept_share, count_pair[:, None]).astype(jnp.bfloat16)
    kept_share, _ = lax.optimization_barrier((kept_share, over_y))
    kept_share = exchange(kept_share.reshape(SPARE, Y, Z * rows).transpose(1, 0, 2), "y")
    pairs = jnp.sum(kept_share[:, SHARE:SHARE + 2, 0].astype(jnp.float32), axis=0)
    scale = -(LOSS_SCALE / (64.0 * pairs[0] + pairs[1]))
    kept_share = kept_share[:, :SHARE].reshape(Y * SHARE, Z * rows)
    kept_hidden = to_all(kept_share, ("x", "c"), V).reshape(V, Y, SHARE, Z * rows)

    def logits_of(features, blocks, here, n):
        total = 0.0
        for away, block in blocks:
            part = lax.dynamic_index_in_dim(features, lax.rem(here + (away + n), n), 0, keepdims=False)
            total = total + lax.dot_general(part, block, across_rows, preferred_element_type=jnp.float32)
        return total

    logits = jnp.concatenate(
        [logits_of(hidden_a, blocks_a, at_y, Y), logits_of(hidden_b, blocks_b, at_z, Z)], axis=1
    )
    logits, kept_hidden, scale = lax.optimization_barrier((logits, kept_hidden, scale))
    local_target = targets - offset
    positions = jnp.arange(cols, dtype=jnp.int32)
    onehot = (positions[None, :] == local_target[:, None]).astype(jnp.float32)
    local_pick = jnp.sum(logits * onehot, axis=1)
    local_top = jnp.max(logits, axis=1)
    shifted = logits - local_top[:, None]
    weights = jnp.exp(shifted)
    stats = jnp.stack(
        [local_top, jnp.sum(weights, axis=1), jnp.sum(weights * shifted, axis=1), local_pick]
    )
    stats = to_all(stats, ("x", "c"), V)
    tops, totals, moments, picks = (stats[:, i] for i in range(4))
    row_top = jnp.max(tops, axis=0)
    lower = tops - row_top[None]
    factor = jnp.exp(lower)
    row_total = jnp.sum(totals * factor, axis=0)
    row_moment = jnp.sum((moments + lower * totals) * factor, axis=0)
    picked = jnp.sum(picks, axis=0)
    entropy = jnp.log(row_total) - row_moment / row_total
    logprob = picked - row_top - jnp.log(row_total)
    slope = surrogate_slope(logprob, old_logprob, advantage, keep_float)
    softmax_rows = jnp.exp(logits - row_top[:, None]) / row_total[:, None]
    logit_grads = (slope[:, None] * (onehot - softmax_rows)).astype(jnp.bfloat16)
    compact = jnp.dot(selector, logit_grads, preferred_element_type=jnp.float32).astype(jnp.bfloat16)

    all_slots = to_all(compact, "y", Y)

    def through(grads, blocks, here, n, dtype):
        parts = jnp.zeros((n, KEEP_MOST, width // n), dtype)
        for away, block in blocks:
            part = lax.dot_general(grads, block, (((1,), (1,)), ((), ())), preferred_element_type=jnp.float32)
            parts = lax.dynamic_update_slice(
                parts, part.astype(dtype)[None], (lax.rem(here + (away + n), n), 0, 0)
            )
        return parts

    parts_a = through(compact[:, :half], blocks_a, at_y, Y, jnp.float32)
    parts_b = through(compact[:, half:], blocks_b, at_z, Z, jnp.bfloat16)
    parts_b = parts_b.reshape(Z, KEEP_MOST, Y, rows).transpose(2, 1, 0, 3).reshape(Y, KEEP_MOST, Z * rows)
    hidden_part = (parts_a + parts_b.astype(jnp.float32)).astype(jnp.bfloat16)

    kept_hidden = kept_hidden.transpose(1, 0, 2, 3).reshape(Y * KEEP_MOST, Z * rows)
    part_head = lax.dot_general(
        kept_hidden, all_slots.reshape(Y * KEEP_MOST, cols),
        (((0,), (0,)), ((), ())), preferred_element_type=jnp.float32,
    ).astype(jnp.bfloat16)
    sums = exchange(part_head.reshape(Z, rows, cols), "z")
    grad_head = jnp.sum(scale * sums.astype(jnp.float32), axis=0)

    hidden_part = hidden_part.reshape(X, C, KEEP_MOST, Z * rows)
    mine = lax.dynamic_index_in_dim(hidden_part, at_c, 1, keepdims=False)
    other = lax.dynamic_index_in_dim(hidden_part, 1 - at_c, 1, keepdims=False)
    pair = mine.astype(jnp.float32) + lax.ppermute(other, "c", [(0, 1), (1, 0)]).astype(jnp.float32)
    total = lax.dynamic_index_in_dim(pair, at_x, 0, keepdims=False)
    for step in range(1, X):
        sent = lax.dynamic_index_in_dim(pair, lax.rem(at_x + step, X), 0, keepdims=False)
        total = total + lax.ppermute(sent, "x", [(i, (i + step) % X) for i in range(X)])
    upper = total.astype(jnp.bfloat16)
    under = (total - upper.astype(jnp.float32)).astype(jnp.bfloat16)
    grad_hidden = scale * lax.dot_general(
        jnp.concatenate([selector, selector]), jnp.concatenate([upper, under]),
        (((0,), (0,)), ((), ())), preferred_element_type=jnp.float32,
    )
    return (entropy, grad_hidden, grad_head)


def solution(mesh):
    grid = Mesh(mesh.devices.reshape(Y, Z, X, C), ("y", "z", "x", "c"))
    dp, vocab = ("y", "z"), ("x", "c")
    placed = (P(dp, None), P(dp, vocab), P(dp), P(dp), P(dp), P(dp))
    return jax.shard_map(
        per_device,
        mesh=grid,
        in_specs=placed,
        out_specs=(P(dp), P(dp, vocab), P(dp, vocab)),
        check_vma=False,
    )
```

```python
import jax
import jax.numpy as jnp
from jax import lax
from jax.experimental import pallas as pl
from jax.experimental.pallas import tpu as pltpu
from jax.sharding import Mesh, PartitionSpec as P

Y, Z, X, C = 8, 8, 4, 2
V = X * C
KEEP_MOST = 80
SPARE = 16
SHARE = KEEP_MOST // V
CLIP_EPS = 0.2
LOSS_SCALE = 8192.0


def surrogate_slope(logprob, old_logprob, advantage, keep_float):
    importance = jnp.exp(logprob - old_logprob)
    bent_term = jnp.tanh((importance - 1.0) / CLIP_EPS)
    clipped = 1.0 + CLIP_EPS * bent_term
    choose_grad = jnp.where(
        importance * advantage <= clipped * advantage,
        advantage,
        advantage * (1.0 - bent_term * bent_term),
    )
    return keep_float * choose_grad * importance


def exchange(parts, axes):
    return lax.all_to_all(parts, axes, split_axis=0, concat_axis=0)


def to_all(values, axes, n):
    return exchange(jnp.broadcast_to(values[None], (n,) + values.shape), axes)


def ring(own, axis, n):
    blocks = [(0, own)]
    up = down = own
    for hop in range(1, n // 2 + 1):
        down = lax.ppermute(down, axis, [(i, (i - 1) % n) for i in range(n)])
        blocks.append((hop, down))
        if hop < n // 2:
            up = lax.ppermute(up, axis, [(i, (i + 1) % n) for i in range(n)])
            blocks.append((-hop, up))
    return blocks


def start_copies(blocks, held, sems):
    copies = [pltpu.make_async_copy(block, held.at[i], sems.at[i]) for i, block in enumerate(blocks)]
    for copy in copies:
        copy.start()
    return copies


def logits_kernel(owners, features_a, features_b, *refs):
    n = (len(refs) - 3) // 2
    out, held, sems = refs[2 * n:]
    half = out.shape[1] // 2
    copies = start_copies(refs[:2 * n], held, sems)
    for first, features in ((0, features_a), (n, features_b)):
        columns = pl.ds(half if first else 0, half)
        for i in range(first, first + n):
            copies[i].wait()
            part = jnp.dot(features[owners[i]], held[i], preferred_element_type=jnp.float32)
            if i == first:
                out[:, columns] = part
            else:
                out[:, columns] += part


def parts_kernel(owners, grads, *refs):
    n = (len(refs) - 4) // 2
    out, held, total, sems = refs[2 * n:]
    half = grads.shape[1] // 2
    rows = out.shape[1] // n
    copies = start_copies(refs[:2 * n], held, sems)
    total[...] = jnp.zeros_like(total)
    over_cols = (((1,), (1,)), ((), ()))
    for i in range(n):
        copies[i].wait()
        total[owners[i]] += lax.dot_general(
            held[i], grads[:, :half], over_cols, preferred_element_type=jnp.float32
        )
    for i in range(n, 2 * n):
        copies[i].wait()
        part = lax.dot_general(held[i], grads[:, half:], over_cols, preferred_element_type=jnp.float32)
        at = pl.ds(pl.multiple_of(owners[i] * rows, rows), rows)
        for y in range(n):
            total[y, at, :] += part[y * rows:(y + 1) * rows]
    out[...] = total[...].astype(out.dtype)


def over_blocks(kernel, out_shape, owners, arrays, blocks, scratch, flops):
    smem, vmem, anywhere = (pl.BlockSpec(memory_space=space) for space in (pltpu.SMEM, pltpu.VMEM, pl.ANY))
    held = pltpu.VMEM((len(blocks),) + blocks[0].shape, blocks[0].dtype)
    moved = len(blocks) * blocks[0].size * 2
    return pl.pallas_call(
        kernel,
        out_shape=out_shape,
        in_specs=[smem] + [vmem] * len(arrays) + [anywhere] * len(blocks),
        out_specs=vmem,
        scratch_shapes=[held, *scratch, pltpu.SemaphoreType.DMA((len(blocks),))],
        compiler_params=pltpu.CompilerParams(vmem_limit_bytes=40 * 1024 * 1024),
        cost_estimate=pl.CostEstimate(flops=flops, bytes_accessed=moved, transcendentals=0),
    )(owners, *arrays, *blocks)


def per_device(hidden, head_weight, targets, kept_mask, old_logprob, advantage):
    tokens, width = hidden.shape
    rows, cols = head_weight.shape
    half = cols // 2
    at_y, at_z, at_x, at_c = (lax.axis_index(name) for name in ("y", "z", "x", "c"))
    at_v = at_x * C + at_c
    offset = at_v * cols

    keep_float = kept_mask.astype(jnp.float32)
    count_rows = jnp.broadcast_to(jnp.sum(keep_float).astype(jnp.bfloat16), (SPARE, half))
    over_z = to_all(jnp.concatenate([head_weight[:, :half], count_rows], axis=0), "z", Z)
    hidden_a = hidden.reshape(tokens, Y, Z * rows).transpose(1, 0, 2)
    hidden_b = hidden.reshape(tokens, Y, Z, rows).transpose(2, 0, 1, 3).reshape(Z, tokens, Y * rows)
    over_z, hidden_a, hidden_b = lax.optimization_barrier((over_z, hidden_a, hidden_b))
    kept_z = jnp.sum(over_z[:, rows, :128].astype(jnp.float32), axis=0)[0]
    head_of_b, _ = lax.optimization_barrier((head_weight[:, half:], over_z))
    over_y = to_all(head_of_b, "y", Y)
    blocks_a = ring(over_z[:, :rows].reshape(Z * rows, half), "y", Y)
    blocks_b = ring(over_y.reshape(Y * rows, half), "z", Z)

    slot_index = jnp.cumsum(kept_mask) - 1
    ids = jnp.arange(KEEP_MOST, dtype=jnp.int32)
    kept = kept_mask[None, :] == 1
    selector = ((slot_index[None, :] == ids[:, None]) & kept).astype(jnp.bfloat16)
    share_ids = jnp.arange(SPARE, dtype=jnp.int32)
    own = (slot_index[None, :] == (at_v * SHARE + share_ids)[:, None]) & kept & (share_ids < SHARE)[:, None]
    kept_share = jnp.dot(own.astype(jnp.bfloat16), hidden, preferred_element_type=jnp.float32)
    high = jnp.floor(kept_z / 64.0)
    count_pair = jnp.where(share_ids == SHARE, high, kept_z - 64.0 * high)
    kept_share = jnp.where(share_ids[:, None] < SHARE, kept_share, count_pair[:, None]).astype(jnp.bfloat16)
    kept_share, _ = lax.optimization_barrier((kept_share, over_y))
    kept_share = exchange(kept_share.reshape(SPARE, Y, Z * rows).transpose(1, 0, 2), "y")
    pairs = jnp.sum(kept_share[:, SHARE:SHARE + 2, 0].astype(jnp.float32), axis=0)
    scale = -(LOSS_SCALE / (64.0 * pairs[0] + pairs[1]))
    kept_share = kept_share[:, :SHARE].reshape(Y * SHARE, Z * rows)
    kept_hidden = to_all(kept_share, ("x", "c"), V).reshape(V, Y, SHARE, Z * rows)

    owners = jnp.stack(
        [lax.rem(at_y + (away + Y), Y) for away, _ in blocks_a] + [lax.rem(at_z + (away + Z), Z) for away, _ in blocks_b]
    ).astype(jnp.int32)
    blocks = [block for _, block in blocks_a + blocks_b]
    logits = over_blocks(
        logits_kernel, jax.ShapeDtypeStruct((tokens, cols), jnp.float32), owners, [hidden_a, hidden_b], blocks, [],
        2 * tokens * width * cols,
    )
    logits, kept_hidden, scale = lax.optimization_barrier((logits, kept_hidden, scale))
    local_target = targets - offset
    positions = jnp.arange(cols, dtype=jnp.int32)
    onehot = (positions[None, :] == local_target[:, None]).astype(jnp.float32)
    local_pick = jnp.sum(logits * onehot, axis=1)
    local_top = jnp.max(logits, axis=1)
    shifted = logits - local_top[:, None]
    weights = jnp.exp(shifted)
    stats = jnp.stack(
        [local_top, jnp.sum(weights, axis=1), jnp.sum(weights * shifted, axis=1), local_pick]
    )
    stats = to_all(stats, ("x", "c"), V)
    tops, totals, moments, picks = (stats[:, i] for i in range(4))
    row_top = jnp.max(tops, axis=0)
    lower = tops - row_top[None]
    factor = jnp.exp(lower)
    row_total = jnp.sum(totals * factor, axis=0)
    row_moment = jnp.sum((moments + lower * totals) * factor, axis=0)
    picked = jnp.sum(picks, axis=0)
    entropy = jnp.log(row_total) - row_moment / row_total
    logprob = picked - row_top - jnp.log(row_total)
    slope = surrogate_slope(logprob, old_logprob, advantage, keep_float)
    softmax_rows = jnp.exp(logits - row_top[:, None]) / row_total[:, None]
    logit_grads = (slope[:, None] * (onehot - softmax_rows)).astype(jnp.bfloat16)
    compact = jnp.dot(selector, logit_grads, preferred_element_type=jnp.float32).astype(jnp.bfloat16)

    all_slots = to_all(compact, "y", Y)

    hidden_part = over_blocks(
        parts_kernel, jax.ShapeDtypeStruct((Y, Z * rows, KEEP_MOST), jnp.bfloat16), owners, [compact], blocks,
        [pltpu.VMEM((Y, Z * rows, KEEP_MOST), jnp.float32)], 2 * KEEP_MOST * width * cols,
    )

    kept_hidden = kept_hidden.transpose(1, 0, 2, 3).reshape(Y * KEEP_MOST, Z * rows)
    part_head = lax.dot_general(
        kept_hidden, all_slots.reshape(Y * KEEP_MOST, cols),
        (((0,), (0,)), ((), ())), preferred_element_type=jnp.float32,
    ).astype(jnp.bfloat16)
    sums = exchange(part_head.reshape(Z, rows, cols), "z")
    grad_head = jnp.sum(scale * sums.astype(jnp.float32), axis=0)

    hidden_part = hidden_part.reshape(X, C, Z * rows, KEEP_MOST)
    mine = lax.dynamic_index_in_dim(hidden_part, at_c, 1, keepdims=False)
    other = lax.dynamic_index_in_dim(hidden_part, 1 - at_c, 1, keepdims=False)
    pair = mine.astype(jnp.float32) + lax.ppermute(other, "c", [(0, 1), (1, 0)]).astype(jnp.float32)
    total = lax.dynamic_index_in_dim(pair, at_x, 0, keepdims=False)
    for step in range(1, X):
        sent = lax.dynamic_index_in_dim(pair, lax.rem(at_x + step, X), 0, keepdims=False)
        total = total + lax.ppermute(sent, "x", [(i, (i + step) % X) for i in range(X)])
    upper = total.astype(jnp.bfloat16)
    under = (total - upper.astype(jnp.float32)).astype(jnp.bfloat16)
    grad_hidden = scale * lax.dot_general(
        jnp.concatenate([selector, selector]), jnp.concatenate([upper, under], axis=1),
        (((0,), (1,)), ((), ())), preferred_element_type=jnp.float32,
    )
    return (entropy, grad_hidden, grad_head)


def solution(mesh):
    grid = Mesh(mesh.devices.reshape(Y, Z, X, C), ("y", "z", "x", "c"))
    dp, vocab = ("y", "z"), ("x", "c")
    placed = (P(dp, None), P(dp, vocab), P(dp), P(dp), P(dp), P(dp))
    return jax.shard_map(
        per_device,
        mesh=grid,
        in_specs=placed,
        out_specs=(P(dp), P(dp, vocab), P(dp, vocab)),
        check_vma=False,
    )
```

```python
import jax
import jax.numpy as jnp
from jax import lax
from jax.sharding import Mesh, PartitionSpec as P

Y, Z, X, C = 8, 8, 4, 2
V = X * C
KEEP_MOST = 80
SPARE = 8
SLOTS = KEEP_MOST + SPARE
SHARE = KEEP_MOST // V
HELD = 16
CLIP_EPS = 0.2
LOSS_SCALE = 8192.0


def surrogate_slope(logprob, old_logprob, advantage, keep_float):
    importance = jnp.exp(logprob - old_logprob)
    bent_term = jnp.tanh((importance - 1.0) / CLIP_EPS)
    clipped = 1.0 + CLIP_EPS * bent_term
    choose_grad = jnp.where(
        importance * advantage <= clipped * advantage,
        advantage,
        advantage * (1.0 - bent_term * bent_term),
    )
    return keep_float * choose_grad * importance


def exchange(parts, axes):
    return lax.all_to_all(parts, axes, split_axis=0, concat_axis=0)


def to_all(values, axes, n):
    return exchange(jnp.broadcast_to(values[None], (n,) + values.shape), axes)


def rows_of(weights, factors):
    positions = lax.broadcasted_iota(jnp.int32, weights.shape, weights.ndim - 1).astype(jnp.float32)
    scale, entry, target = (factors[..., i, :, None] for i in range(3))
    return jnp.where(positions == target, entry, -scale * weights.astype(jnp.float32)).astype(jnp.bfloat16)


def per_device(hidden, head_weight, targets, kept_mask, old_logprob, advantage):
    tokens, width = hidden.shape
    rows, cols = head_weight.shape
    offset = (lax.axis_index("x") * C + lax.axis_index("c")) * cols
    head = lax.all_gather(head_weight, ("y", "z"), axis=0, tiled=True)

    keep_float = kept_mask.astype(jnp.float32)
    slot_index = jnp.cumsum(kept_mask) - 1
    ids = jnp.arange(SLOTS, dtype=jnp.int32)
    kept = kept_mask[None, :] == 1
    chosen = (slot_index[None, :] == ids[:, None]) & kept
    selector = chosen.astype(jnp.bfloat16)
    share_ids = jnp.arange(HELD, dtype=jnp.int32)
    first = (lax.axis_index("x") * C + lax.axis_index("c")) * SHARE
    own = (slot_index[None, :] == (first + share_ids)[:, None]) & kept & (share_ids < SHARE)[:, None]
    kept_hidden = jnp.dot(own.astype(jnp.bfloat16), hidden, preferred_element_type=jnp.float32)
    kept_hidden = jnp.where(share_ids[:, None] < SHARE, kept_hidden, jnp.sum(keep_float)).astype(jnp.bfloat16)
    kept_hidden = exchange(kept_hidden.reshape(HELD, Y, Z * rows).transpose(1, 0, 2), "y")
    kept_y = jnp.sum(kept_hidden[:, SHARE, :128].astype(jnp.float32), axis=0)
    kept_hidden = to_all(kept_hidden, ("x", "c"), V)[:, :, :SHARE]
    kept_hidden = kept_hidden.transpose(1, 0, 2, 3).reshape(Y, KEEP_MOST, Z * rows)
    kept_total = jnp.sum(to_all(jnp.broadcast_to(kept_y, (8, 128)), "z", Z), axis=0)[0, 0]
    scale = -(LOSS_SCALE / kept_total)
    hidden, kept_hidden, scale = lax.optimization_barrier((hidden, kept_hidden, scale))

    logits = jnp.dot(hidden, head, preferred_element_type=jnp.float32)
    local_target = targets - offset
    positions = jnp.arange(cols, dtype=jnp.int32)
    hit = positions[None, :] == local_target[:, None]
    local_top = jnp.max(logits, axis=1)
    shifted = logits - local_top[:, None]
    weights = jnp.exp(shifted)

    compact = jnp.dot(
        selector, jnp.where(hit, 0.0, weights).astype(jnp.bfloat16), preferred_element_type=jnp.float32
    ).astype(jnp.bfloat16)
    all_slots = lax.all_gather(compact, "y")

    stats = jnp.stack(
        [
            local_top,
            jnp.sum(weights, axis=1),
            jnp.sum(weights * shifted, axis=1),
            jnp.sum(jnp.where(hit, logits, 0.0), axis=1),
        ]
    )
    stats, compact = lax.optimization_barrier((stats, compact))
    stats = lax.all_gather(stats, ("x", "c"))
    tops, totals, moments, picks = (stats[:, i] for i in range(4))
    row_top = jnp.max(tops, axis=0)
    lower = tops - row_top[None]
    factor = jnp.exp(lower)
    row_total = jnp.sum(totals * factor, axis=0)
    row_moment = jnp.sum((moments + lower * totals) * factor, axis=0)
    picked = jnp.sum(picks, axis=0)
    entropy = jnp.log(row_total) - row_moment / row_total
    logprob = picked - row_top - jnp.log(row_total)
    slope = surrogate_slope(logprob, old_logprob, advantage, keep_float)
    row_scale = slope * (jnp.exp(local_top - row_top) / row_total)
    row_entry = slope * (1.0 - jnp.exp(picked - row_top) / row_total)
    of_slots = jnp.stack([row_scale, row_entry, local_target.astype(jnp.float32)])
    of_slots = jnp.sum(jnp.where(chosen[None], of_slots[:, None, :], 0.0), axis=2)

    all_factors = to_all(jnp.pad(of_slots, ((0, 5), (0, 128 - SLOTS))), "y", Y)

    own_rows = rows_of(compact, of_slots)
    hidden_part = lax.dot_general(
        own_rows, head, (((1,), (1,)), ((), ())), preferred_element_type=jnp.float32
    ).astype(jnp.bfloat16)[:KEEP_MOST]
    mine = width // V
    hidden_part = hidden_part.reshape(KEEP_MOST, V, mine).transpose(1, 0, 2)
    hidden_part, all_factors = lax.optimization_barrier((hidden_part, all_factors))
    hidden_part = exchange(hidden_part, ("x", "c"))

    all_rows = rows_of(all_slots[:, :KEEP_MOST], all_factors[:, :3, :KEEP_MOST])
    part_head = lax.dot_general(
        kept_hidden.reshape(Y * KEEP_MOST, Z * rows), all_rows.reshape(Y * KEEP_MOST, cols), (((0,), (0,)), ((), ())),
        preferred_element_type=jnp.float32,
    ).astype(jnp.bfloat16)
    sums = exchange(part_head.reshape(Z, rows, cols), "z")
    grad_head = scale * jnp.sum(sums.astype(jnp.float32), axis=0)

    spread = jnp.tile(selector[:KEEP_MOST], (V, 1))
    grad_hidden = scale * lax.dot_general(
        spread, hidden_part.reshape(V * KEEP_MOST, mine), (((0,), (0,)), ((), ())),
        preferred_element_type=jnp.float32,
    )
    return (entropy, grad_hidden, grad_head)


def solution(mesh):
    grid = Mesh(mesh.devices.reshape(Y, Z, X, C), ("y", "z", "x", "c"))
    dp, vocab = ("y", "z"), ("x", "c")
    placed = (P(dp, None), P(dp, vocab), P(dp), P(dp), P(dp), P(dp))
    return jax.shard_map(
        per_device,
        mesh=grid,
        in_specs=placed,
        out_specs=(P(dp), P(dp, vocab), P(dp, vocab)),
        check_vma=False,
    )
```

```python
import jax
import jax.numpy as jnp
from jax import lax
from jax.sharding import Mesh, PartitionSpec as P

Y, Z, X, C = 8, 8, 4, 2
V = X * C
KEEP_MOST = 80
SPARE = 8
SLOTS = KEEP_MOST + SPARE
SHARE = KEEP_MOST // V
HELD = 16
CLIP_EPS = 0.2
LOSS_SCALE = 8192.0


def surrogate_slope(logprob, old_logprob, advantage, keep_float):
    importance = jnp.exp(logprob - old_logprob)
    bent_term = jnp.tanh((importance - 1.0) / CLIP_EPS)
    clipped = 1.0 + CLIP_EPS * bent_term
    choose_grad = jnp.where(
        importance * advantage <= clipped * advantage,
        advantage,
        advantage * (1.0 - bent_term * bent_term),
    )
    return keep_float * choose_grad * importance


def exchange(parts, axes):
    return lax.all_to_all(parts, axes, split_axis=0, concat_axis=0)


def to_all(values, axes, n):
    return exchange(jnp.broadcast_to(values[None], (n,) + values.shape), axes)


def rows_of(weights, factors):
    positions = lax.broadcasted_iota(jnp.int32, weights.shape, weights.ndim - 1).astype(jnp.float32)
    scale, entry, target = (factors[..., i, :, None] for i in range(3))
    return jnp.where(positions == target, entry, -scale * weights.astype(jnp.float32)).astype(jnp.bfloat16)


def per_device(hidden, head_weight, targets, kept_mask, old_logprob, advantage):
    tokens, width = hidden.shape
    rows, cols = head_weight.shape
    offset = (lax.axis_index("x") * C + lax.axis_index("c")) * cols
    head = lax.all_gather(head_weight, ("y", "z"), axis=0, tiled=True)

    keep_float = kept_mask.astype(jnp.float32)
    slot_index = jnp.cumsum(kept_mask) - 1
    ids = jnp.arange(SLOTS, dtype=jnp.int32)
    kept = kept_mask[None, :] == 1
    chosen = (slot_index[None, :] == ids[:, None]) & kept
    selector = chosen.astype(jnp.bfloat16)
    share_ids = jnp.arange(HELD, dtype=jnp.int32)
    first = (lax.axis_index("x") * C + lax.axis_index("c")) * SHARE
    own = (slot_index[None, :] == (first + share_ids)[:, None]) & kept & (share_ids < SHARE)[:, None]
    kept_hidden = jnp.dot(own.astype(jnp.bfloat16), hidden, preferred_element_type=jnp.float32)
    kept_hidden = jnp.where(share_ids[:, None] < SHARE, kept_hidden, jnp.sum(keep_float)).astype(jnp.bfloat16)
    kept_hidden = exchange(kept_hidden.reshape(HELD, Y, Z * rows).transpose(1, 0, 2), "y")
    kept_y = jnp.sum(kept_hidden[:, SHARE, :128].astype(jnp.float32), axis=0)
    kept_hidden = to_all(kept_hidden, ("x", "c"), V)[:, :, :SHARE]
    kept_hidden = kept_hidden.transpose(1, 0, 2, 3).reshape(Y, KEEP_MOST, Z * rows)
    kept_total = jnp.sum(to_all(jnp.broadcast_to(kept_y, (8, 128)), "z", Z), axis=0)[0, 0]
    scale = -(LOSS_SCALE / kept_total)
    hidden, kept_hidden, scale = lax.optimization_barrier((hidden, kept_hidden, scale))

    logits = jnp.dot(hidden, head, preferred_element_type=jnp.float32)
    local_target = targets - offset
    positions = jnp.arange(cols, dtype=jnp.int32)
    hit = positions[None, :] == local_target[:, None]
    local_top = jnp.max(logits, axis=1)
    shifted = logits - local_top[:, None]
    weights = jnp.exp(shifted)

    compact = jnp.dot(
        selector, jnp.where(hit, 0.0, weights).astype(jnp.bfloat16), preferred_element_type=jnp.float32
    ).astype(jnp.bfloat16)
    all_slots = lax.all_gather(compact, "y")

    stats = jnp.stack(
        [
            local_top,
            jnp.sum(weights, axis=1),
            jnp.sum(weights * shifted, axis=1),
            jnp.sum(jnp.where(hit, logits, 0.0), axis=1),
        ]
    )
    stats, compact = lax.optimization_barrier((stats, compact))
    stats = lax.all_gather(stats, ("x", "c"))
    tops, totals, moments, picks = (stats[:, i] for i in range(4))
    row_top = jnp.max(tops, axis=0)
    lower = tops - row_top[None]
    factor = jnp.exp(lower)
    row_total = jnp.sum(totals * factor, axis=0)
    row_moment = jnp.sum((moments + lower * totals) * factor, axis=0)
    picked = jnp.sum(picks, axis=0)
    entropy = jnp.log(row_total) - row_moment / row_total
    logprob = picked - row_top - jnp.log(row_total)
    slope = surrogate_slope(logprob, old_logprob, advantage, keep_float)
    row_scale = slope * (jnp.exp(local_top - row_top) / row_total)
    row_entry = slope * (1.0 - jnp.exp(picked - row_top) / row_total)
    of_slots = jnp.stack([row_scale, row_entry, local_target.astype(jnp.float32)])
    of_slots = jnp.sum(jnp.where(chosen[None], of_slots[:, None, :], 0.0), axis=2)

    all_factors = to_all(jnp.pad(of_slots, ((0, 5), (0, 128 - SLOTS))), "y", Y)

    own_rows = rows_of(compact, of_slots)
    hidden_part = lax.dot_general(
        own_rows, head, (((1,), (1,)), ((), ())), preferred_element_type=jnp.float32
    ).astype(jnp.bfloat16)[:KEEP_MOST]

    all_rows = rows_of(all_slots[:, :KEEP_MOST], all_factors[:, :3, :KEEP_MOST])
    part_head = lax.dot_general(
        kept_hidden.reshape(Y * KEEP_MOST, Z * rows), all_rows.reshape(Y * KEEP_MOST, cols), (((0,), (0,)), ((), ())),
        preferred_element_type=jnp.float32,
    ).astype(jnp.bfloat16)
    hidden_part, part_head = lax.optimization_barrier((hidden_part, part_head))
    sums = exchange(part_head.reshape(Z, rows, cols), "z")
    grad_head = scale * jnp.sum(sums.astype(jnp.float32), axis=0)

    hidden_part = hidden_part.reshape(KEEP_MOST, X, C, width // V).transpose(1, 2, 0, 3)
    at_x, at_c = lax.axis_index("x"), lax.axis_index("c")
    mine = lax.dynamic_index_in_dim(hidden_part, at_c, 1, keepdims=False)
    other = lax.dynamic_index_in_dim(hidden_part, 1 - at_c, 1, keepdims=False)
    pair = mine.astype(jnp.float32) + lax.ppermute(other, "c", [(0, 1), (1, 0)]).astype(jnp.float32)
    total = lax.dynamic_index_in_dim(pair, at_x, 0, keepdims=False)
    for step in range(1, X):
        sent = lax.dynamic_index_in_dim(pair, lax.rem(at_x + step, X), 0, keepdims=False)
        total = total + lax.ppermute(sent, "x", [(i, (i + step) % X) for i in range(X)])
    upper = total.astype(jnp.bfloat16)
    under = (total - upper.astype(jnp.float32)).astype(jnp.bfloat16)
    grad_hidden = scale * lax.dot_general(
        jnp.concatenate([selector[:KEEP_MOST]] * 2), jnp.concatenate([upper, under]),
        (((0,), (0,)), ((), ())), preferred_element_type=jnp.float32,
    )
    return (entropy, grad_hidden, grad_head)


def solution(mesh):
    grid = Mesh(mesh.devices.reshape(Y, Z, X, C), ("y", "z", "x", "c"))
    dp, vocab = ("y", "z"), ("x", "c")
    placed = (P(dp, None), P(dp, vocab), P(dp), P(dp), P(dp), P(dp))
    return jax.shard_map(
        per_device,
        mesh=grid,
        in_specs=placed,
        out_specs=(P(dp), P(dp, vocab), P(dp, vocab)),
        check_vma=False,
    )
```

```python
import jax
import jax.numpy as jnp
from jax import lax
from jax.sharding import Mesh, PartitionSpec as P

Y, Z, X, C = 8, 8, 4, 2
V = X * C
KEEP_MOST = 80
SPARE = 8
SLOTS = KEEP_MOST + SPARE
SHARE = KEEP_MOST // V
HELD = 16
CLIP_EPS = 0.2
LOSS_SCALE = 8192.0


def surrogate_slope(logprob, old_logprob, advantage, keep_float):
    importance = jnp.exp(logprob - old_logprob)
    bent_term = jnp.tanh((importance - 1.0) / CLIP_EPS)
    clipped = 1.0 + CLIP_EPS * bent_term
    choose_grad = jnp.where(
        importance * advantage <= clipped * advantage,
        advantage,
        advantage * (1.0 - bent_term * bent_term),
    )
    return keep_float * choose_grad * importance


def exchange(parts, axes):
    return lax.all_to_all(parts, axes, split_axis=0, concat_axis=0)


def to_all(values, axes, n):
    return exchange(jnp.broadcast_to(values[None], (n,) + values.shape), axes)


def rows_of(weights, factors):
    positions = lax.broadcasted_iota(jnp.int32, weights.shape, weights.ndim - 1).astype(jnp.float32)
    scale, entry, target = (factors[..., i, :, None] for i in range(3))
    return jnp.where(positions == target, entry, -scale * weights.astype(jnp.float32)).astype(jnp.bfloat16)


def per_device(hidden, head_weight, targets, kept_mask, old_logprob, advantage):
    tokens, width = hidden.shape
    rows, cols = head_weight.shape
    offset = (lax.axis_index("x") * C + lax.axis_index("c")) * cols
    head = lax.all_gather(head_weight, ("y", "z"), axis=0, tiled=True)

    keep_float = kept_mask.astype(jnp.float32)
    slot_index = jnp.cumsum(kept_mask) - 1
    ids = jnp.arange(SLOTS, dtype=jnp.int32)
    kept = kept_mask[None, :] == 1
    chosen = (slot_index[None, :] == ids[:, None]) & kept
    selector = chosen.astype(jnp.bfloat16)
    share_ids = jnp.arange(HELD, dtype=jnp.int32)
    first = (lax.axis_index("x") * C + lax.axis_index("c")) * SHARE
    own = (slot_index[None, :] == (first + share_ids)[:, None]) & kept & (share_ids < SHARE)[:, None]
    kept_hidden = jnp.dot(own.astype(jnp.bfloat16), hidden, preferred_element_type=jnp.float32)
    kept_hidden = jnp.where(share_ids[:, None] < SHARE, kept_hidden, jnp.sum(keep_float)).astype(jnp.bfloat16)
    kept_hidden = exchange(kept_hidden.reshape(HELD, Y, Z * rows).transpose(1, 0, 2), "y")
    kept_y = jnp.sum(kept_hidden[:, SHARE, :128].astype(jnp.float32), axis=0)
    kept_hidden = to_all(kept_hidden, ("x", "c"), V)[:, :, :SHARE]
    kept_hidden = kept_hidden.transpose(1, 0, 2, 3).reshape(Y, KEEP_MOST, Z * rows)
    kept_total = jnp.sum(to_all(jnp.broadcast_to(kept_y, (8, 128)), "z", Z), axis=0)[0, 0]
    scale = -(LOSS_SCALE / kept_total)
    hidden, kept_hidden, scale = lax.optimization_barrier((hidden, kept_hidden, scale))

    logits = jnp.dot(hidden, head, preferred_element_type=jnp.float32)
    local_target = targets - offset
    positions = jnp.arange(cols, dtype=jnp.int32)
    hit = positions[None, :] == local_target[:, None]
    local_top = jnp.max(logits, axis=1)
    shifted = logits - local_top[:, None]
    weights = jnp.exp(shifted)

    compact = jnp.dot(
        selector, jnp.where(hit, 0.0, weights).astype(jnp.bfloat16), preferred_element_type=jnp.float32
    ).astype(jnp.bfloat16)
    all_slots = lax.all_gather(compact, "y")

    stats = jnp.stack(
        [
            local_top,
            jnp.sum(weights, axis=1),
            jnp.sum(weights * shifted, axis=1),
            jnp.sum(jnp.where(hit, logits, 0.0), axis=1),
        ]
    )
    stats, compact = lax.optimization_barrier((stats, compact))
    stats = lax.all_gather(stats, ("x", "c"))
    tops, totals, moments, picks = (stats[:, i] for i in range(4))
    row_top = jnp.max(tops, axis=0)
    lower = tops - row_top[None]
    factor = jnp.exp(lower)
    row_total = jnp.sum(totals * factor, axis=0)
    row_moment = jnp.sum((moments + lower * totals) * factor, axis=0)
    picked = jnp.sum(picks, axis=0)
    entropy = jnp.log(row_total) - row_moment / row_total
    logprob = picked - row_top - jnp.log(row_total)
    slope = surrogate_slope(logprob, old_logprob, advantage, keep_float)
    row_scale = slope * (jnp.exp(local_top - row_top) / row_total)
    row_entry = slope * (1.0 - jnp.exp(picked - row_top) / row_total)
    of_slots = jnp.stack([row_scale, row_entry, local_target.astype(jnp.float32)])
    of_slots = jnp.sum(jnp.where(chosen[None], of_slots[:, None, :], 0.0), axis=2)

    all_factors = to_all(jnp.pad(of_slots, ((0, 5), (0, 128 - SLOTS))), "y", Y)

    own_rows = rows_of(compact, of_slots)
    hidden_part = lax.dot_general(
        own_rows, head, (((1,), (1,)), ((), ())), preferred_element_type=jnp.float32
    ).astype(jnp.bfloat16)[:KEEP_MOST]

    hidden_part, all_factors = lax.optimization_barrier((hidden_part, all_factors))
    hidden_part = hidden_part.reshape(KEEP_MOST, V, width // V).transpose(1, 0, 2)
    hidden_part = hidden_part.reshape(X, C, KEEP_MOST, width // V)
    at_x, at_c = lax.axis_index("x"), lax.axis_index("c")
    mine = lax.dynamic_index_in_dim(hidden_part, at_c, 1, keepdims=False)
    other = lax.dynamic_index_in_dim(hidden_part, 1 - at_c, 1, keepdims=False)
    pair = mine.astype(jnp.float32) + lax.ppermute(other, "c", [(0, 1), (1, 0)]).astype(jnp.float32)

    all_rows = rows_of(all_slots[:, :KEEP_MOST], all_factors[:, :3, :KEEP_MOST])
    part_head = lax.dot_general(
        kept_hidden.reshape(Y * KEEP_MOST, Z * rows), all_rows.reshape(Y * KEEP_MOST, cols), (((0,), (0,)), ((), ())),
        preferred_element_type=jnp.float32,
    ).astype(jnp.bfloat16)
    pair, part_head = lax.optimization_barrier((pair, part_head))
    sums = exchange(part_head.reshape(Z, rows, cols), "z")
    grad_head = scale * jnp.sum(sums.astype(jnp.float32), axis=0)

    total = lax.dynamic_index_in_dim(pair, at_x, 0, keepdims=False)
    for step in range(1, X):
        sent = lax.dynamic_index_in_dim(pair, lax.rem(at_x + step, X), 0, keepdims=False)
        total = total + lax.ppermute(sent, "x", [(i, (i + step) % X) for i in range(X)])
    upper = total.astype(jnp.bfloat16)
    under = (total - upper.astype(jnp.float32)).astype(jnp.bfloat16)
    grad_hidden = scale * lax.dot_general(
        jnp.concatenate([selector[:KEEP_MOST]] * 2), jnp.concatenate([upper, under]),
        (((0,), (0,)), ((), ())), preferred_element_type=jnp.float32,
    )
    return (entropy, grad_hidden, grad_head)


def solution(mesh):
    grid = Mesh(mesh.devices.reshape(Y, Z, X, C), ("y", "z", "x", "c"))
    dp, vocab = ("y", "z"), ("x", "c")
    placed = (P(dp, None), P(dp, vocab), P(dp), P(dp), P(dp), P(dp))
    return jax.shard_map(
        per_device,
        mesh=grid,
        in_specs=placed,
        out_specs=(P(dp), P(dp, vocab), P(dp, vocab)),
        check_vma=False,
    )
```

```python
import jax
import jax.numpy as jnp
from jax import lax
from jax.sharding import Mesh, PartitionSpec as P

Y, Z, X, C = 8, 8, 4, 2
V = X * C
KEEP_MOST = 80
SPARE = 8
SLOTS = KEEP_MOST + SPARE
SHARE = KEEP_MOST // V
HELD = 16
SENT = 512
CLIP_EPS = 0.2
LOSS_SCALE = 8192.0


def surrogate_slope(logprob, old_logprob, advantage, keep_float):
    importance = jnp.exp(logprob - old_logprob)
    bent_term = jnp.tanh((importance - 1.0) / CLIP_EPS)
    clipped = 1.0 + CLIP_EPS * bent_term
    choose_grad = jnp.where(
        importance * advantage <= clipped * advantage,
        advantage,
        advantage * (1.0 - bent_term * bent_term),
    )
    return keep_float * choose_grad * importance


def exchange(parts, axes):
    return lax.all_to_all(parts, axes, split_axis=0, concat_axis=0)


def to_all(values, axes, n):
    return exchange(jnp.broadcast_to(values[None], (n,) + values.shape), axes)


def shift(block, step):
    return lax.ppermute(block, "y", [(i, (i + step) % Y) for i in range(Y)])


def ring_over_y(own):
    here = lax.axis_index("y")
    whole = jnp.zeros((Y,) + own.shape, own.dtype)

    def put(whole, block, away):
        return lax.dynamic_update_slice(whole, block[None], (lax.rem(here + (away + Y), Y), 0, 0))

    whole = put(whole, own, 0)
    up = down = own
    for hop in range(1, Y // 2 + 1):
        down = shift(down, -1)
        whole = put(whole, down, hop)
        if hop < Y // 2:
            up = shift(up, 1)
            whole = put(whole, up, -hop)
    return whole, down


def rows_of(weights, factors):
    positions = lax.broadcasted_iota(jnp.int32, weights.shape, weights.ndim - 1).astype(jnp.float32)
    scale, entry, target = (factors[..., i, :, None] for i in range(3))
    return jnp.where(positions == target, entry, -scale * weights.astype(jnp.float32)).astype(jnp.bfloat16)


def per_device(hidden, head_weight, targets, kept_mask, old_logprob, advantage):
    tokens, width = hidden.shape
    rows, cols = head_weight.shape
    offset = (lax.axis_index("x") * C + lax.axis_index("c")) * cols

    head_a = lax.all_gather(head_weight[:, :SENT], ("y", "z"), axis=0, tiled=True)
    keep_float = kept_mask.astype(jnp.float32)
    count_rows = jnp.broadcast_to(jnp.sum(keep_float).astype(jnp.bfloat16), (HELD, cols - SENT))
    over_z = to_all(jnp.concatenate([head_weight[:, SENT:], count_rows], axis=0), "z", Z)
    kept_z = jnp.sum(over_z[:, rows, :128].astype(jnp.float32), axis=0)[0]
    head_b, last = ring_over_y(over_z[:, :rows].reshape(Z * rows, cols - SENT))
    head_b = head_b.reshape(width, cols - SENT)

    slot_index = jnp.cumsum(kept_mask) - 1
    ids = jnp.arange(SLOTS, dtype=jnp.int32)
    kept = kept_mask[None, :] == 1
    chosen = (slot_index[None, :] == ids[:, None]) & kept
    selector = chosen.astype(jnp.bfloat16)
    share_ids = jnp.arange(HELD, dtype=jnp.int32)
    first = (lax.axis_index("x") * C + lax.axis_index("c")) * SHARE
    own = (slot_index[None, :] == (first + share_ids)[:, None]) & kept & (share_ids < SHARE)[:, None]
    kept_hidden = jnp.dot(own.astype(jnp.bfloat16), hidden, preferred_element_type=jnp.float32)
    high = jnp.floor(kept_z / 64.0)
    count_pair = jnp.where(share_ids == SHARE, high, kept_z - 64.0 * high)
    kept_hidden = jnp.where(share_ids[:, None] < SHARE, kept_hidden, count_pair[:, None]).astype(jnp.bfloat16)
    kept_hidden = kept_hidden.reshape(HELD, Y, Z * rows).transpose(1, 0, 2)
    kept_hidden, _ = lax.optimization_barrier((kept_hidden, last))
    kept_share = exchange(kept_hidden, "y")
    pairs = jnp.sum(kept_share[:, SHARE:SHARE + 2, 0].astype(jnp.float32), axis=0)
    scale = -(LOSS_SCALE / (64.0 * pairs[0] + pairs[1]))
    kept_hidden = to_all(kept_share, ("x", "c"), V)[:, :, :SHARE]
    kept_hidden = kept_hidden.transpose(1, 0, 2, 3).reshape(Y, KEEP_MOST, Z * rows)
    hidden, scale = lax.optimization_barrier((hidden, scale))

    logits = jnp.concatenate(
        [
            jnp.dot(hidden, head_a, preferred_element_type=jnp.float32),
            jnp.dot(hidden, head_b, preferred_element_type=jnp.float32),
        ],
        axis=1,
    )
    local_target = targets - offset
    positions = jnp.arange(cols, dtype=jnp.int32)
    hit = positions[None, :] == local_target[:, None]
    local_top = jnp.max(logits, axis=1)
    shifted = logits - local_top[:, None]
    weights = jnp.exp(shifted)

    compact = jnp.dot(
        selector, jnp.where(hit, 0.0, weights).astype(jnp.bfloat16), preferred_element_type=jnp.float32
    ).astype(jnp.bfloat16)
    all_slots = lax.all_gather(compact, "y")

    stats = jnp.stack(
        [
            local_top,
            jnp.sum(weights, axis=1),
            jnp.sum(weights * shifted, axis=1),
            jnp.sum(jnp.where(hit, logits, 0.0), axis=1),
        ]
    )
    stats, compact, kept_hidden = lax.optimization_barrier((stats, compact, kept_hidden))
    stats = to_all(stats, ("x", "c"), V)
    tops, totals, moments, picks = (stats[:, i] for i in range(4))
    row_top = jnp.max(tops, axis=0)
    lower = tops - row_top[None]
    factor = jnp.exp(lower)
    row_total = jnp.sum(totals * factor, axis=0)
    row_moment = jnp.sum((moments + lower * totals) * factor, axis=0)
    picked = jnp.sum(picks, axis=0)
    entropy = jnp.log(row_total) - row_moment / row_total
    logprob = picked - row_top - jnp.log(row_total)
    slope = surrogate_slope(logprob, old_logprob, advantage, keep_float)
    row_scale = slope * (jnp.exp(local_top - row_top) / row_total)
    row_entry = slope * (1.0 - jnp.exp(picked - row_top) / row_total)
    of_slots = jnp.stack([row_scale, row_entry, local_target.astype(jnp.float32)])
    of_slots = jnp.sum(jnp.where(chosen[None], of_slots[:, None, :], 0.0), axis=2)

    all_factors = to_all(jnp.pad(of_slots, ((0, 5), (0, 128 - SLOTS))), "y", Y)

    own_rows = rows_of(compact, of_slots)
    over_cols = (((1,), (1,)), ((), ()))
    hidden_part = (
        lax.dot_general(own_rows[:, :SENT], head_a, over_cols, preferred_element_type=jnp.float32)
        + lax.dot_general(own_rows[:, SENT:], head_b, over_cols, preferred_element_type=jnp.float32)
    ).astype(jnp.bfloat16)[:KEEP_MOST]

    hidden_part, all_factors = lax.optimization_barrier((hidden_part, all_factors))
    hidden_part = hidden_part.reshape(KEEP_MOST, V, width // V).transpose(1, 0, 2)
    hidden_part = hidden_part.reshape(X, C, KEEP_MOST, width // V)
    at_x, at_c = lax.axis_index("x"), lax.axis_index("c")
    mine = lax.dynamic_index_in_dim(hidden_part, at_c, 1, keepdims=False)
    other = lax.dynamic_index_in_dim(hidden_part, 1 - at_c, 1, keepdims=False)
    pair = mine.astype(jnp.float32) + lax.ppermute(other, "c", [(0, 1), (1, 0)]).astype(jnp.float32)

    all_rows = rows_of(all_slots[:, :KEEP_MOST], all_factors[:, :3, :KEEP_MOST])
    part_head = lax.dot_general(
        kept_hidden.reshape(Y * KEEP_MOST, Z * rows), all_rows.reshape(Y * KEEP_MOST, cols), (((0,), (0,)), ((), ())),
        preferred_element_type=jnp.float32,
    ).astype(jnp.bfloat16)
    pair, part_head = lax.optimization_barrier((pair, part_head))
    sums = exchange(part_head.reshape(Z, rows, cols), "z")
    grad_head = scale * jnp.sum(sums.astype(jnp.float32), axis=0)

    total = lax.dynamic_index_in_dim(pair, at_x, 0, keepdims=False)
    for step in range(1, X):
        sent = lax.dynamic_index_in_dim(pair, lax.rem(at_x + step, X), 0, keepdims=False)
        total = total + lax.ppermute(sent, "x", [(i, (i + step) % X) for i in range(X)])
    upper = total.astype(jnp.bfloat16)
    under = (total - upper.astype(jnp.float32)).astype(jnp.bfloat16)
    grad_hidden = scale * lax.dot_general(
        jnp.concatenate([selector[:KEEP_MOST]] * 2), jnp.concatenate([upper, under]),
        (((0,), (0,)), ((), ())), preferred_element_type=jnp.float32,
    )
    return (entropy, grad_hidden, grad_head)


def solution(mesh):
    grid = Mesh(mesh.devices.reshape(Y, Z, X, C), ("y", "z", "x", "c"))
    dp, vocab = ("y", "z"), ("x", "c")
    placed = (P(dp, None), P(dp, vocab), P(dp), P(dp), P(dp), P(dp))
    return jax.shard_map(
        per_device,
        mesh=grid,
        in_specs=placed,
        out_specs=(P(dp), P(dp, vocab), P(dp, vocab)),
        check_vma=False,
    )
```

```python
import jax
import jax.numpy as jnp
from jax import lax
from jax.experimental import pallas as pl
from jax.experimental.pallas import tpu as pltpu
from jax.sharding import Mesh, PartitionSpec as P

Y, Z, X, C = 8, 8, 4, 2
V = X * C
KEEP_MOST = 80
SPARE = 16
SLOTS = KEEP_MOST + SPARE
SHARE = KEEP_MOST // V
HELD = 16
BLOCKS = 8
GROUP = 32
CLIP_EPS = 0.2
LOSS_SCALE = 8192.0


def surrogate_slope(logprob, old_logprob, advantage, keep_float):
    importance = jnp.exp(logprob - old_logprob)
    bent_term = jnp.tanh((importance - 1.0) / CLIP_EPS)
    clipped = 1.0 + CLIP_EPS * bent_term
    choose_grad = jnp.where(
        importance * advantage <= clipped * advantage,
        advantage,
        advantage * (1.0 - bent_term * bent_term),
    )
    return keep_float * choose_grad * importance


def exchange(parts, axes):
    return lax.all_to_all(parts, axes, split_axis=0, concat_axis=0)


def to_all(values, axes, n):
    return exchange(jnp.broadcast_to(values[None], (n,) + values.shape), axes)


def rows_of(weights, factors):
    positions = lax.broadcasted_iota(jnp.int32, weights.shape, weights.ndim - 1).astype(jnp.float32)
    scale, entry, target = (factors[..., i, :, None] for i in range(3))
    return jnp.where(positions == target, entry, -scale * weights.astype(jnp.float32)).astype(jnp.bfloat16)


def softmax_kernel(hidden, target, selector, head, compact, stats, held, total, weights_held, sems):
    depth = held.shape[1]
    copies = [
        pltpu.make_async_copy(head.at[pl.ds(i * depth, depth)], held.at[i], sems.at[i]) for i in range(BLOCKS)
    ]
    for copy in copies:
        copy.start()
    for i, copy in enumerate(copies):
        copy.wait()
        part = jnp.dot(hidden[:, i * depth:(i + 1) * depth], held[i], preferred_element_type=jnp.float32)
        total[...] = total[...] + part if i else part
    tokens, cols = total.shape
    positions = lax.broadcasted_iota(jnp.int32, (GROUP, cols), 1)
    lane = lax.broadcasted_iota(jnp.int32, (GROUP, stats.shape[1]), 1)
    for first in range(0, tokens, GROUP):
        group = pl.ds(first, GROUP)
        logits = total[group]
        hit = positions == target[group]
        top = jnp.max(logits, axis=1, keepdims=True)
        shifted = logits - top
        weights = jnp.exp(shifted)
        weights_held[group] = jnp.where(hit, 0.0, weights).astype(jnp.bfloat16)
        sums = [weights, weights * shifted, jnp.where(hit, logits, 0.0)]
        sums = [jnp.sum(values, axis=1, keepdims=True) for values in sums]
        stats[group] = jnp.where(
            lane == 0, top, jnp.where(lane == 1, sums[0], jnp.where(lane == 2, sums[1], sums[2]))
        )
    compact[...] = jnp.dot(
        selector[...], weights_held[...], preferred_element_type=jnp.float32
    ).astype(jnp.bfloat16)


def softmax_of(hidden, target, selector, head):
    tokens, width = hidden.shape
    cols = head.shape[1]
    vmem, anywhere = pl.BlockSpec(memory_space=pltpu.VMEM), pl.BlockSpec(memory_space=pl.ANY)
    return pl.pallas_call(
        softmax_kernel,
        out_shape=(
            jax.ShapeDtypeStruct((SLOTS, cols), jnp.bfloat16),
            jax.ShapeDtypeStruct((tokens, 128), jnp.float32),
        ),
        in_specs=[vmem, vmem, vmem, anywhere],
        out_specs=(vmem, vmem),
        scratch_shapes=[
            pltpu.VMEM((BLOCKS, width // BLOCKS, cols), jnp.bfloat16),
            pltpu.VMEM((tokens, cols), jnp.float32),
            pltpu.VMEM((tokens, cols), jnp.bfloat16),
            pltpu.SemaphoreType.DMA((BLOCKS,)),
        ],
        compiler_params=pltpu.CompilerParams(vmem_limit_bytes=58 * 1024 * 1024),
        cost_estimate=pl.CostEstimate(
            flops=2 * tokens * width * cols, bytes_accessed=width * (cols + tokens) * 2, transcendentals=tokens * cols
        ),
    )(hidden, target, selector, head)


def per_device(hidden, head_weight, targets, kept_mask, old_logprob, advantage):
    tokens, width = hidden.shape
    rows, cols = head_weight.shape
    offset = (lax.axis_index("x") * C + lax.axis_index("c")) * cols
    head = lax.all_gather(head_weight, ("y", "z"), axis=0, tiled=True)

    keep_float = kept_mask.astype(jnp.float32)
    slot_index = jnp.cumsum(kept_mask) - 1
    ids = jnp.arange(SLOTS, dtype=jnp.int32)
    kept = kept_mask[None, :] == 1
    chosen = (slot_index[None, :] == ids[:, None]) & kept
    selector = chosen.astype(jnp.bfloat16)
    share_ids = jnp.arange(HELD, dtype=jnp.int32)
    first = (lax.axis_index("x") * C + lax.axis_index("c")) * SHARE
    own = (slot_index[None, :] == (first + share_ids)[:, None]) & kept & (share_ids < SHARE)[:, None]
    kept_hidden = jnp.dot(own.astype(jnp.bfloat16), hidden, preferred_element_type=jnp.float32)
    kept_hidden = jnp.where(share_ids[:, None] < SHARE, kept_hidden, jnp.sum(keep_float)).astype(jnp.bfloat16)
    kept_hidden = exchange(kept_hidden.reshape(HELD, Y, Z * rows).transpose(1, 0, 2), "y")
    kept_y = jnp.sum(kept_hidden[:, SHARE, :128].astype(jnp.float32), axis=0)
    kept_hidden = to_all(kept_hidden, ("x", "c"), V)[:, :, :SHARE]
    kept_hidden = kept_hidden.transpose(1, 0, 2, 3).reshape(Y, KEEP_MOST, Z * rows)
    kept_total = jnp.sum(to_all(jnp.broadcast_to(kept_y, (8, 128)), "z", Z), axis=0)[0, 0]
    scale = -(LOSS_SCALE / kept_total)
    hidden, kept_hidden, scale = lax.optimization_barrier((hidden, kept_hidden, scale))

    local_target = targets - offset
    compact, stats = softmax_of(hidden, local_target[:, None], selector, head)
    stats = stats[:, :4].T
    local_top = stats[0]

    all_slots = lax.all_gather(compact, "y")

    stats, compact = lax.optimization_barrier((stats, compact))
    stats = lax.all_gather(stats, ("x", "c"))
    tops, totals, moments, picks = (stats[:, i] for i in range(4))
    row_top = jnp.max(tops, axis=0)
    lower = tops - row_top[None]
    factor = jnp.exp(lower)
    row_total = jnp.sum(totals * factor, axis=0)
    row_moment = jnp.sum((moments + lower * totals) * factor, axis=0)
    picked = jnp.sum(picks, axis=0)
    entropy = jnp.log(row_total) - row_moment / row_total
    logprob = picked - row_top - jnp.log(row_total)
    slope = surrogate_slope(logprob, old_logprob, advantage, keep_float)
    row_scale = slope * (jnp.exp(local_top - row_top) / row_total)
    row_entry = slope * (1.0 - jnp.exp(picked - row_top) / row_total)
    of_slots = jnp.stack([row_scale, row_entry, local_target.astype(jnp.float32)])
    of_slots = jnp.sum(jnp.where(chosen[None], of_slots[:, None, :], 0.0), axis=2)

    all_factors = to_all(jnp.pad(of_slots, ((0, 5), (0, 128 - SLOTS))), "y", Y)

    own_rows = rows_of(compact, of_slots)
    hidden_part = lax.dot_general(
        own_rows, head, (((1,), (1,)), ((), ())), preferred_element_type=jnp.float32
    ).astype(jnp.bfloat16)[:KEEP_MOST]

    hidden_part, all_factors = lax.optimization_barrier((hidden_part, all_factors))
    hidden_part = hidden_part.reshape(KEEP_MOST, V, width // V).transpose(1, 0, 2)
    hidden_part = hidden_part.reshape(X, C, KEEP_MOST, width // V)
    at_x, at_c = lax.axis_index("x"), lax.axis_index("c")
    mine = lax.dynamic_index_in_dim(hidden_part, at_c, 1, keepdims=False)
    other = lax.dynamic_index_in_dim(hidden_part, 1 - at_c, 1, keepdims=False)
    pair = mine.astype(jnp.float32) + lax.ppermute(other, "c", [(0, 1), (1, 0)]).astype(jnp.float32)

    all_rows = rows_of(all_slots[:, :KEEP_MOST], all_factors[:, :3, :KEEP_MOST])
    part_head = scale * lax.dot_general(
        kept_hidden, all_rows, (((0, 1), (0, 1)), ((), ())), preferred_element_type=jnp.float32
    )
    part_head = part_head.astype(jnp.bfloat16)
    pair, part_head = lax.optimization_barrier((pair, part_head))
    sums = exchange(part_head.reshape(Z, rows, cols), "z")
    grad_head = jnp.sum(sums.astype(jnp.float32), axis=0)

    total = lax.dynamic_index_in_dim(pair, at_x, 0, keepdims=False)
    for step in range(1, X):
        sent = lax.dynamic_index_in_dim(pair, lax.rem(at_x + step, X), 0, keepdims=False)
        total = total + lax.ppermute(sent, "x", [(i, (i + step) % X) for i in range(X)])
    upper = total.astype(jnp.bfloat16)
    under = (total - upper.astype(jnp.float32)).astype(jnp.bfloat16)
    grad_hidden = scale * lax.dot_general(
        jnp.concatenate([selector[:KEEP_MOST]] * 2), jnp.concatenate([upper, under]),
        (((0,), (0,)), ((), ())), preferred_element_type=jnp.float32,
    )
    return (entropy, grad_hidden, grad_head)


def solution(mesh):
    grid = Mesh(mesh.devices.reshape(Y, Z, X, C), ("y", "z", "x", "c"))
    dp, vocab = ("y", "z"), ("x", "c")
    placed = (P(dp, None), P(dp, vocab), P(dp), P(dp), P(dp), P(dp))
    return jax.shard_map(
        per_device,
        mesh=grid,
        in_specs=placed,
        out_specs=(P(dp), P(dp, vocab), P(dp, vocab)),
        check_vma=False,
    )
```

```python
import jax
import jax.numpy as jnp
from jax import lax
from jax.sharding import Mesh, PartitionSpec as P

Y, Z, X, C = 8, 8, 4, 2
V = X * C
KEEP_MOST = 80
SPARE = 8
SLOTS = KEEP_MOST + SPARE
SHARE = KEEP_MOST // V
HELD = 16
CLIP_EPS = 0.2
LOSS_SCALE = 8192.0


def surrogate_slope(logprob, old_logprob, advantage, keep_float):
    importance = jnp.exp(logprob - old_logprob)
    bent_term = jnp.tanh((importance - 1.0) / CLIP_EPS)
    clipped = 1.0 + CLIP_EPS * bent_term
    choose_grad = jnp.where(
        importance * advantage <= clipped * advantage,
        advantage,
        advantage * (1.0 - bent_term * bent_term),
    )
    return keep_float * choose_grad * importance


def exchange(parts, axes):
    return lax.all_to_all(parts, axes, split_axis=0, concat_axis=0)


def to_all(values, axes, n):
    return exchange(jnp.broadcast_to(values[None], (n,) + values.shape), axes)


def rows_of(weights, factors):
    positions = lax.broadcasted_iota(jnp.int32, weights.shape, weights.ndim - 1).astype(jnp.float32)
    scale, entry, target = (factors[..., i, :, None] for i in range(3))
    return jnp.where(positions == target, entry, -scale * weights.astype(jnp.float32)).astype(jnp.bfloat16)


def per_device(hidden, head_weight, targets, kept_mask, old_logprob, advantage):
    tokens, width = hidden.shape
    rows, cols = head_weight.shape
    offset = (lax.axis_index("x") * C + lax.axis_index("c")) * cols
    head = lax.all_gather(head_weight, ("y", "z"), axis=0, tiled=True)

    keep_float = kept_mask.astype(jnp.float32)
    slot_index = jnp.cumsum(kept_mask) - 1
    ids = jnp.arange(SLOTS, dtype=jnp.int32)
    kept = kept_mask[None, :] == 1
    chosen = (slot_index[None, :] == ids[:, None]) & kept
    selector = chosen.astype(jnp.bfloat16)
    share_ids = jnp.arange(HELD, dtype=jnp.int32)
    first = (lax.axis_index("x") * C + lax.axis_index("c")) * SHARE
    own = (slot_index[None, :] == (first + share_ids)[:, None]) & kept & (share_ids < SHARE)[:, None]
    kept_hidden = jnp.dot(own.astype(jnp.bfloat16), hidden, preferred_element_type=jnp.float32)
    kept_hidden = jnp.where(share_ids[:, None] < SHARE, kept_hidden, jnp.sum(keep_float)).astype(jnp.bfloat16)
    kept_hidden = exchange(kept_hidden.reshape(HELD, Y, Z * rows).transpose(1, 0, 2), "y")
    kept_y = jnp.sum(kept_hidden[:, SHARE, :128].astype(jnp.float32), axis=0)
    kept_hidden = to_all(kept_hidden, ("x", "c"), V)[:, :, :SHARE]
    kept_hidden = kept_hidden.transpose(1, 0, 2, 3).reshape(Y, KEEP_MOST, Z * rows)
    kept_total = jnp.sum(to_all(jnp.broadcast_to(kept_y, (8, 128)), "z", Z), axis=0)[0, 0]
    scale = -(LOSS_SCALE / kept_total)
    hidden, kept_hidden, scale = lax.optimization_barrier((hidden, kept_hidden, scale))

    logits = jnp.dot(hidden, head, preferred_element_type=jnp.float32)
    local_target = targets - offset
    positions = jnp.arange(cols, dtype=jnp.int32)
    hit = positions[None, :] == local_target[:, None]
    local_top = jnp.max(logits, axis=1)
    shifted = logits - local_top[:, None]
    weights = jnp.exp(shifted)

    compact = jnp.dot(
        selector, jnp.where(hit, 0.0, weights).astype(jnp.bfloat16), preferred_element_type=jnp.float32
    ).astype(jnp.bfloat16)
    all_slots = lax.all_gather(compact, "y")

    stats = jnp.stack(
        [
            local_top,
            jnp.sum(weights, axis=1),
            jnp.sum(weights * shifted, axis=1),
            jnp.sum(jnp.where(hit, logits, 0.0), axis=1),
        ]
    )
    stats, compact = lax.optimization_barrier((stats, compact))
    stats = lax.all_gather(stats, ("x", "c"))
    tops, totals, moments, picks = (stats[:, i] for i in range(4))
    row_top = jnp.max(tops, axis=0)
    lower = tops - row_top[None]
    factor = jnp.exp(lower)
    row_total = jnp.sum(totals * factor, axis=0)
    row_moment = jnp.sum((moments + lower * totals) * factor, axis=0)
    picked = jnp.sum(picks, axis=0)
    entropy = jnp.log(row_total) - row_moment / row_total
    logprob = picked - row_top - jnp.log(row_total)
    slope = surrogate_slope(logprob, old_logprob, advantage, keep_float)
    row_scale = slope * (jnp.exp(local_top - row_top) / row_total)
    row_entry = slope * (1.0 - jnp.exp(picked - row_top) / row_total)
    of_slots = jnp.stack([row_scale, row_entry, local_target.astype(jnp.float32)])
    of_slots = jnp.sum(jnp.where(chosen[None], of_slots[:, None, :], 0.0), axis=2)

    all_factors = to_all(jnp.pad(of_slots, ((0, 5), (0, 128 - SLOTS))), "y", Y)

    own_rows = rows_of(compact, of_slots)
    hidden_part = lax.dot_general(
        own_rows, head, (((1,), (1,)), ((), ())), preferred_element_type=jnp.float32
    ).astype(jnp.bfloat16)[:KEEP_MOST]

    hidden_part, all_factors = lax.optimization_barrier((hidden_part, all_factors))
    hidden_part = hidden_part.reshape(KEEP_MOST, V, width // V).transpose(1, 0, 2)
    hidden_part = hidden_part.reshape(X, C, KEEP_MOST, width // V)
    at_x, at_c = lax.axis_index("x"), lax.axis_index("c")
    mine = lax.dynamic_index_in_dim(hidden_part, at_c, 1, keepdims=False)
    other = lax.dynamic_index_in_dim(hidden_part, 1 - at_c, 1, keepdims=False)
    pair = mine.astype(jnp.float32) + lax.ppermute(other, "c", [(0, 1), (1, 0)]).astype(jnp.float32)

    all_rows = rows_of(all_slots[:, :KEEP_MOST], all_factors[:, :3, :KEEP_MOST])
    part_head = scale * lax.dot_general(
        kept_hidden, all_rows, (((0, 1), (0, 1)), ((), ())), preferred_element_type=jnp.float32
    )
    part_head = part_head.astype(jnp.bfloat16)
    pair, part_head = lax.optimization_barrier((pair, part_head))
    sums = exchange(part_head.reshape(Z, rows, cols), "z")
    grad_head = jnp.sum(sums.astype(jnp.float32), axis=0)

    total = lax.dynamic_index_in_dim(pair, at_x, 0, keepdims=False)
    for step in range(1, X):
        sent = lax.dynamic_index_in_dim(pair, lax.rem(at_x + step, X), 0, keepdims=False)
        total = total + lax.ppermute(sent, "x", [(i, (i + step) % X) for i in range(X)])
    upper = total.astype(jnp.bfloat16)
    under = (total - upper.astype(jnp.float32)).astype(jnp.bfloat16)
    grad_hidden = scale * lax.dot_general(
        jnp.concatenate([selector[:KEEP_MOST]] * 2), jnp.concatenate([upper, under]),
        (((0,), (0,)), ((), ())), preferred_element_type=jnp.float32,
    )
    return (entropy, grad_hidden, grad_head)


def solution(mesh):
    grid = Mesh(mesh.devices.reshape(Y, Z, X, C), ("y", "z", "x", "c"))
    dp, vocab = ("y", "z"), ("x", "c")
    placed = (P(dp, None), P(dp, vocab), P(dp), P(dp), P(dp), P(dp))
    return jax.shard_map(
        per_device,
        mesh=grid,
        in_specs=placed,
        out_specs=(P(dp), P(dp, vocab), P(dp, vocab)),
        check_vma=False,
    )
```

```python
import jax
import jax.numpy as jnp
from jax import lax
from jax.experimental import pallas as pl
from jax.experimental.pallas import tpu as pltpu
from jax.sharding import Mesh, PartitionSpec as P

Y, Z, X, C = 8, 8, 4, 2
V = X * C
KEEP_MOST = 80
SPARE = 16
SLOTS = KEEP_MOST + SPARE
SHARE = KEEP_MOST // V
HELD = 16
CLIP_EPS = 0.2
LOSS_SCALE = 8192.0


def surrogate_slope(logprob, old_logprob, advantage, keep_float):
    importance = jnp.exp(logprob - old_logprob)
    bent_term = jnp.tanh((importance - 1.0) / CLIP_EPS)
    clipped = 1.0 + CLIP_EPS * bent_term
    choose_grad = jnp.where(
        importance * advantage <= clipped * advantage,
        advantage,
        advantage * (1.0 - bent_term * bent_term),
    )
    return keep_float * choose_grad * importance


def exchange(parts, axes):
    return lax.all_to_all(parts, axes, split_axis=0, concat_axis=0)


def to_all(values, axes, n):
    return exchange(jnp.broadcast_to(values[None], (n,) + values.shape), axes)


def rows_of(weights, factors):
    positions = lax.broadcasted_iota(jnp.int32, weights.shape, weights.ndim - 1).astype(jnp.float32)
    scale, entry, target = (factors[..., i, :, None] for i in range(3))
    return jnp.where(positions == target, entry, -scale * weights.astype(jnp.float32)).astype(jnp.bfloat16)


def product_kernel(features, slots, factors, out, held):
    positions = lax.broadcasted_iota(jnp.int32, (KEEP_MOST, slots.shape[2]), 1).astype(jnp.float32)
    for y in range(Y):
        scale, entry, target = (factors[y, :, i:i + 1] for i in range(3))
        weights = slots[y, :KEEP_MOST, :].astype(jnp.float32)
        held[y * KEEP_MOST:(y + 1) * KEEP_MOST, :] = jnp.where(
            positions == target, entry, -scale * weights
        ).astype(held.dtype)
    out[...] = jnp.dot(features[...], held[...], preferred_element_type=jnp.float32).astype(out.dtype)


def product_of(features, slots, factors):
    rows, cols = features.shape[0], slots.shape[2]
    vmem = pl.BlockSpec(memory_space=pltpu.VMEM)
    return pl.pallas_call(
        product_kernel,
        out_shape=jax.ShapeDtypeStruct((rows, cols), jnp.bfloat16),
        in_specs=[vmem] * 3,
        out_specs=vmem,
        scratch_shapes=[pltpu.VMEM((Y * KEEP_MOST, cols), jnp.bfloat16)],
        compiler_params=pltpu.CompilerParams(vmem_limit_bytes=58 * 1024 * 1024),
        cost_estimate=pl.CostEstimate(
            flops=2 * rows * Y * KEEP_MOST * cols, bytes_accessed=2 * slots.size + 4 * rows * cols, transcendentals=0
        ),
    )(features, slots, factors)


def per_device(hidden, head_weight, targets, kept_mask, old_logprob, advantage):
    tokens, width = hidden.shape
    rows, cols = head_weight.shape
    offset = (lax.axis_index("x") * C + lax.axis_index("c")) * cols
    head = lax.all_gather(head_weight, ("y", "z"), axis=0, tiled=True)

    keep_float = kept_mask.astype(jnp.float32)
    slot_index = jnp.cumsum(kept_mask) - 1
    ids = jnp.arange(SLOTS, dtype=jnp.int32)
    kept = kept_mask[None, :] == 1
    chosen = (slot_index[None, :] == ids[:, None]) & kept
    selector = chosen.astype(jnp.bfloat16)
    share_ids = jnp.arange(HELD, dtype=jnp.int32)
    first = (lax.axis_index("x") * C + lax.axis_index("c")) * SHARE
    own = (slot_index[None, :] == (first + share_ids)[:, None]) & kept & (share_ids < SHARE)[:, None]
    kept_hidden = jnp.dot(own.astype(jnp.bfloat16), hidden, preferred_element_type=jnp.float32)
    kept_hidden = jnp.where(share_ids[:, None] < SHARE, kept_hidden, jnp.sum(keep_float)).astype(jnp.bfloat16)
    kept_hidden = exchange(kept_hidden.reshape(HELD, Y, Z * rows).transpose(1, 0, 2), "y")
    kept_y = jnp.sum(kept_hidden[:, SHARE, :128].astype(jnp.float32), axis=0)
    kept_hidden = to_all(kept_hidden, ("x", "c"), V)[:, :, :SHARE]
    kept_hidden = kept_hidden.transpose(1, 0, 2, 3).reshape(Y * KEEP_MOST, Z * rows).T
    kept_total = jnp.sum(to_all(jnp.broadcast_to(kept_y, (8, 128)), "z", Z), axis=0)[0, 0]
    scale = -(LOSS_SCALE / kept_total)
    hidden, kept_hidden, scale = lax.optimization_barrier((hidden, kept_hidden, scale))

    logits = jnp.dot(hidden, head, preferred_element_type=jnp.float32)
    local_target = targets - offset
    positions = jnp.arange(cols, dtype=jnp.int32)
    hit = positions[None, :] == local_target[:, None]
    local_top = jnp.max(logits, axis=1)
    shifted = logits - local_top[:, None]
    weights = jnp.exp(shifted)

    compact = jnp.dot(
        selector, jnp.where(hit, 0.0, weights).astype(jnp.bfloat16), preferred_element_type=jnp.float32
    ).astype(jnp.bfloat16)
    all_slots = lax.all_gather(compact, "y")

    stats = jnp.stack(
        [
            local_top,
            jnp.sum(weights, axis=1),
            jnp.sum(weights * shifted, axis=1),
            jnp.sum(jnp.where(hit, logits, 0.0), axis=1),
        ]
    )
    stats, compact = lax.optimization_barrier((stats, compact))
    stats = lax.all_gather(stats, ("x", "c"))
    tops, totals, moments, picks = (stats[:, i] for i in range(4))
    row_top = jnp.max(tops, axis=0)
    lower = tops - row_top[None]
    factor = jnp.exp(lower)
    row_total = jnp.sum(totals * factor, axis=0)
    row_moment = jnp.sum((moments + lower * totals) * factor, axis=0)
    picked = jnp.sum(picks, axis=0)
    entropy = jnp.log(row_total) - row_moment / row_total
    logprob = picked - row_top - jnp.log(row_total)
    slope = surrogate_slope(logprob, old_logprob, advantage, keep_float)
    row_scale = slope * (jnp.exp(local_top - row_top) / row_total)
    row_entry = slope * (1.0 - jnp.exp(picked - row_top) / row_total)
    of_slots = jnp.stack([row_scale, row_entry, local_target.astype(jnp.float32)])
    of_slots = jnp.sum(jnp.where(chosen[None], of_slots[:, None, :], 0.0), axis=2)

    all_factors = to_all(jnp.pad(of_slots, ((0, 5), (0, 128 - SLOTS))), "y", Y)

    own_rows = rows_of(compact, of_slots)
    hidden_part = lax.dot_general(
        own_rows, head, (((1,), (1,)), ((), ())), preferred_element_type=jnp.float32
    ).astype(jnp.bfloat16)[:KEEP_MOST]

    hidden_part, all_factors = lax.optimization_barrier((hidden_part, all_factors))
    hidden_part = hidden_part.reshape(KEEP_MOST, V, width // V).transpose(1, 0, 2)
    hidden_part = hidden_part.reshape(X, C, KEEP_MOST, width // V)
    at_x, at_c = lax.axis_index("x"), lax.axis_index("c")
    mine = lax.dynamic_index_in_dim(hidden_part, at_c, 1, keepdims=False)
    other = lax.dynamic_index_in_dim(hidden_part, 1 - at_c, 1, keepdims=False)
    pair = mine.astype(jnp.float32) + lax.ppermute(other, "c", [(0, 1), (1, 0)]).astype(jnp.float32)

    factors = jnp.stack([scale * all_factors[:, 0], scale * all_factors[:, 1], all_factors[:, 2]], axis=2)
    part_head = product_of(kept_hidden, all_slots, factors[:, :KEEP_MOST])
    pair, part_head = lax.optimization_barrier((pair, part_head))
    sums = exchange(part_head.reshape(Z, rows, cols), "z")
    grad_head = jnp.sum(sums.astype(jnp.float32), axis=0)

    total = lax.dynamic_index_in_dim(pair, at_x, 0, keepdims=False)
    for step in range(1, X):
        sent = lax.dynamic_index_in_dim(pair, lax.rem(at_x + step, X), 0, keepdims=False)
        total = total + lax.ppermute(sent, "x", [(i, (i + step) % X) for i in range(X)])
    upper = total.astype(jnp.bfloat16)
    under = (total - upper.astype(jnp.float32)).astype(jnp.bfloat16)
    grad_hidden = scale * lax.dot_general(
        jnp.concatenate([selector[:KEEP_MOST]] * 2), jnp.concatenate([upper, under]),
        (((0,), (0,)), ((), ())), preferred_element_type=jnp.float32,
    )
    return (entropy, grad_hidden, grad_head)


def solution(mesh):
    grid = Mesh(mesh.devices.reshape(Y, Z, X, C), ("y", "z", "x", "c"))
    dp, vocab = ("y", "z"), ("x", "c")
    placed = (P(dp, None), P(dp, vocab), P(dp), P(dp), P(dp), P(dp))
    return jax.shard_map(
        per_device,
        mesh=grid,
        in_specs=placed,
        out_specs=(P(dp), P(dp, vocab), P(dp, vocab)),
        check_vma=False,
    )
```

```python
import jax
import jax.numpy as jnp
from jax import lax
from jax.experimental import pallas as pl
from jax.experimental.pallas import tpu as pltpu
from jax.sharding import Mesh, PartitionSpec as P

Y, Z, X, C = 8, 8, 4, 2
V = X * C
KEEP_MOST = 80
SPARE = 16
SLOTS = KEEP_MOST + SPARE
SHARE = KEEP_MOST // V
HELD = 16
CLIP_EPS = 0.2
LOSS_SCALE = 8192.0


def surrogate_slope(logprob, old_logprob, advantage, keep_float):
    importance = jnp.exp(logprob - old_logprob)
    bent_term = jnp.tanh((importance - 1.0) / CLIP_EPS)
    clipped = 1.0 + CLIP_EPS * bent_term
    choose_grad = jnp.where(
        importance * advantage <= clipped * advantage,
        advantage,
        advantage * (1.0 - bent_term * bent_term),
    )
    return keep_float * choose_grad * importance


def exchange(parts, axes):
    return lax.all_to_all(parts, axes, split_axis=0, concat_axis=0)


def to_all(values, axes, n):
    return exchange(jnp.broadcast_to(values[None], (n,) + values.shape), axes)


def rows_of(weights, factors):
    positions = lax.broadcasted_iota(jnp.int32, weights.shape, weights.ndim - 1).astype(jnp.float32)
    scale, entry, target = (factors[..., i, :, None] for i in range(3))
    return jnp.where(positions == target, entry, -scale * weights.astype(jnp.float32)).astype(jnp.bfloat16)


def product_kernel(features, slots, factors, out, held):
    positions = lax.broadcasted_iota(jnp.int32, (KEEP_MOST, slots.shape[2]), 1).astype(jnp.float32)
    for y in range(Y):
        scale, entry, target = (factors[y, :, i:i + 1] for i in range(3))
        weights = slots[y, :KEEP_MOST, :].astype(jnp.float32)
        held[y * KEEP_MOST:(y + 1) * KEEP_MOST, :] = jnp.where(
            positions == target, entry, -scale * weights
        ).astype(held.dtype)
    out[...] = jnp.dot(features[...], held[...], preferred_element_type=jnp.float32).astype(out.dtype)


def product_of(features, slots, factors):
    rows, cols = features.shape[0], slots.shape[2]
    vmem = pl.BlockSpec(memory_space=pltpu.VMEM)
    return pl.pallas_call(
        product_kernel,
        out_shape=jax.ShapeDtypeStruct((rows, cols), jnp.bfloat16),
        in_specs=[vmem] * 3,
        out_specs=vmem,
        scratch_shapes=[pltpu.VMEM((Y * KEEP_MOST, cols), jnp.bfloat16)],
        compiler_params=pltpu.CompilerParams(vmem_limit_bytes=58 * 1024 * 1024),
        cost_estimate=pl.CostEstimate(
            flops=2 * rows * Y * KEEP_MOST * cols, bytes_accessed=2 * slots.size + 4 * rows * cols, transcendentals=0
        ),
    )(features, slots, factors)


def sum_kernel(parts, out):
    total = parts[0].astype(jnp.float32)
    for i in range(1, parts.shape[0]):
        total = total + parts[i].astype(jnp.float32)
    out[...] = total


def sum_of(parts):
    n, rows, cols = parts.shape
    half = cols // 2
    return pl.pallas_call(
        sum_kernel,
        out_shape=jax.ShapeDtypeStruct((rows, cols), jnp.float32),
        grid=(2,),
        in_specs=[pl.BlockSpec((n, rows, half), lambda i: (0, 0, i))],
        out_specs=pl.BlockSpec((rows, half), lambda i: (0, i)),
        compiler_params=pltpu.CompilerParams(vmem_limit_bytes=58 * 1024 * 1024),
        cost_estimate=pl.CostEstimate(flops=parts.size, bytes_accessed=2 * parts.size + 4 * rows * cols, transcendentals=0),
    )(parts)


def per_device(hidden, head_weight, targets, kept_mask, old_logprob, advantage):
    tokens, width = hidden.shape
    rows, cols = head_weight.shape
    offset = (lax.axis_index("x") * C + lax.axis_index("c")) * cols
    head = lax.all_gather(head_weight, ("y", "z"), axis=0, tiled=True)

    keep_float = kept_mask.astype(jnp.float32)
    slot_index = jnp.cumsum(kept_mask) - 1
    ids = jnp.arange(SLOTS, dtype=jnp.int32)
    kept = kept_mask[None, :] == 1
    chosen = (slot_index[None, :] == ids[:, None]) & kept
    selector = chosen.astype(jnp.bfloat16)
    share_ids = jnp.arange(HELD, dtype=jnp.int32)
    first = (lax.axis_index("x") * C + lax.axis_index("c")) * SHARE
    own = (slot_index[None, :] == (first + share_ids)[:, None]) & kept & (share_ids < SHARE)[:, None]
    kept_hidden = jnp.dot(own.astype(jnp.bfloat16), hidden, preferred_element_type=jnp.float32)
    kept_hidden = jnp.where(share_ids[:, None] < SHARE, kept_hidden, jnp.sum(keep_float)).astype(jnp.bfloat16)
    kept_hidden = exchange(kept_hidden.reshape(HELD, Y, Z * rows).transpose(1, 0, 2), "y")
    kept_y = jnp.sum(kept_hidden[:, SHARE, :128].astype(jnp.float32), axis=0)
    kept_hidden = to_all(kept_hidden, ("x", "c"), V)[:, :, :SHARE]
    kept_hidden = kept_hidden.transpose(1, 0, 2, 3).reshape(Y * KEEP_MOST, Z * rows).T
    kept_total = jnp.sum(to_all(jnp.broadcast_to(kept_y, (8, 128)), "z", Z), axis=0)[0, 0]
    scale = -(LOSS_SCALE / kept_total)
    hidden, kept_hidden, scale = lax.optimization_barrier((hidden, kept_hidden, scale))

    logits = jnp.dot(hidden, head, preferred_element_type=jnp.float32)
    local_target = targets - offset
    positions = jnp.arange(cols, dtype=jnp.int32)
    hit = positions[None, :] == local_target[:, None]
    local_top = jnp.max(logits, axis=1)
    shifted = logits - local_top[:, None]
    weights = jnp.exp(shifted)

    compact = jnp.dot(
        selector, jnp.where(hit, 0.0, weights).astype(jnp.bfloat16), preferred_element_type=jnp.float32
    ).astype(jnp.bfloat16)
    all_slots = lax.all_gather(compact, "y")

    stats = jnp.stack(
        [
            local_top,
            jnp.sum(weights, axis=1),
            jnp.sum(weights * shifted, axis=1),
            jnp.sum(jnp.where(hit, logits, 0.0), axis=1),
        ]
    )
    stats, compact = lax.optimization_barrier((stats, compact))
    stats = lax.all_gather(stats, ("x", "c"))
    tops, totals, moments, picks = (stats[:, i] for i in range(4))
    row_top = jnp.max(tops, axis=0)
    lower = tops - row_top[None]
    factor = jnp.exp(lower)
    row_total = jnp.sum(totals * factor, axis=0)
    row_moment = jnp.sum((moments + lower * totals) * factor, axis=0)
    picked = jnp.sum(picks, axis=0)
    entropy = jnp.log(row_total) - row_moment / row_total
    logprob = picked - row_top - jnp.log(row_total)
    slope = surrogate_slope(logprob, old_logprob, advantage, keep_float)
    row_scale = slope * (jnp.exp(local_top - row_top) / row_total)
    row_entry = slope * (1.0 - jnp.exp(picked - row_top) / row_total)
    of_slots = jnp.stack([row_scale, row_entry, local_target.astype(jnp.float32)])
    of_slots = jnp.sum(jnp.where(chosen[None], of_slots[:, None, :], 0.0), axis=2)

    all_factors = to_all(jnp.pad(of_slots, ((0, 5), (0, 128 - SLOTS))), "y", Y)

    own_rows = rows_of(compact, of_slots)
    hidden_part = lax.dot_general(
        own_rows, head, (((1,), (1,)), ((), ())), preferred_element_type=jnp.float32
    ).astype(jnp.bfloat16)[:KEEP_MOST]

    hidden_part, all_factors = lax.optimization_barrier((hidden_part, all_factors))
    hidden_part = hidden_part.reshape(KEEP_MOST, V, width // V).transpose(1, 0, 2)
    hidden_part = hidden_part.reshape(X, C, KEEP_MOST, width // V)
    at_x, at_c = lax.axis_index("x"), lax.axis_index("c")
    mine = lax.dynamic_index_in_dim(hidden_part, at_c, 1, keepdims=False)
    other = lax.dynamic_index_in_dim(hidden_part, 1 - at_c, 1, keepdims=False)
    pair = mine.astype(jnp.float32) + lax.ppermute(other, "c", [(0, 1), (1, 0)]).astype(jnp.float32)

    factors = jnp.stack([scale * all_factors[:, 0], scale * all_factors[:, 1], all_factors[:, 2]], axis=2)
    part_head = product_of(kept_hidden, all_slots, factors[:, :KEEP_MOST])
    pair, part_head = lax.optimization_barrier((pair, part_head))
    sums = exchange(part_head.reshape(Z, rows, cols), "z")
    grad_head = sum_of(sums)

    total = lax.dynamic_index_in_dim(pair, at_x, 0, keepdims=False)
    for step in range(1, X):
        sent = lax.dynamic_index_in_dim(pair, lax.rem(at_x + step, X), 0, keepdims=False)
        total = total + lax.ppermute(sent, "x", [(i, (i + step) % X) for i in range(X)])
    upper = total.astype(jnp.bfloat16)
    under = (total - upper.astype(jnp.float32)).astype(jnp.bfloat16)
    grad_hidden = scale * lax.dot_general(
        jnp.concatenate([selector[:KEEP_MOST]] * 2), jnp.concatenate([upper, under]),
        (((0,), (0,)), ((), ())), preferred_element_type=jnp.float32,
    )
    return (entropy, grad_hidden, grad_head)


def solution(mesh):
    grid = Mesh(mesh.devices.reshape(Y, Z, X, C), ("y", "z", "x", "c"))
    dp, vocab = ("y", "z"), ("x", "c")
    placed = (P(dp, None), P(dp, vocab), P(dp), P(dp), P(dp), P(dp))
    return jax.shard_map(
        per_device,
        mesh=grid,
        in_specs=placed,
        out_specs=(P(dp), P(dp, vocab), P(dp, vocab)),
        check_vma=False,
    )
```
